512 devices in a mesh: ctx: 32 (over z, x_hi), tp: 16 (over x_lo, y, core).
Axes of the slice: x: 4 (x_hi: 2, x_lo: 2; x = x_hi * 2 + x_lo), y: 4, z: 16, core: 2. Of those that a mesh axis runs over, the one named last changes fastest.
Arguments:
- token_ids: int32 [2, 16384], P(None, 'ctx'), may hold values from 0 to 511
- lengths: int32 [2], replicated, may hold values from 8192 to 16384, as said below
- embedding: bfloat16 [512, 8192], P(None, 'tp'), may hold values from -6 to 6
- query_act: bfloat16 [2, 16384, 8192], P(None, 'ctx', 'tp'), may hold values from -11 to 11
- key_act: bfloat16 [2, 16384, 8192], P(None, 'ctx', 'tp'), may hold values from -6 to 6
- value_act: bfloat16 [2, 16384, 8192], P(None, 'ctx', 'tp'), may hold values from -6 to 6
- short_filter: bfloat16 [512, 128], P('tp'), may hold values from -0.5 to 0.5
- decay_rates: float32 [512, 16], P('tp'), may hold values from 0 to 1
- residues: float32 [512, 16], P('tp'), may hold values from -1 to 1
- skip_gain: float32 [8192], P('tp'), may hold values from 0.5 to 1.5
- norm_gain: float32 [8192], P('tp'), may hold values from 0.25 to 1.75
Outputs:
- scored: bfloat16 [2, 16384, 8192], P(None, 'ctx', 'tp')
The draws below stay inside these ranges and needn't reach their ends.
Inputs may be any that keep to these rules, and one draw needn't show every extreme that they name: `lengths`: one sample has the full length 16384.
All inputs are finite; a program needn't handle non-finite values.
Results may differ from the reference program's by a relative error of at most 0.0065.
Values may be sent and summed in bfloat16 or wider, within the bound.
No kernel may reach another device: no remote copies, remote signals or barrier semaphores. Data moves between devices by JAX's collectives and lax.ppermute only.
A program may use at most 64 MiB of HBM per device.

```python
import math
import jax
import jax.numpy as jnp
import numpy as np
from jax import lax

D = 8192
V = 512
TAPS = 128
GROUP = 16
MODES = 16
SAMPLES = 2
SEQ = 16384
GROUPS = 512


def decay_pair(key):
    base_key = jax.random.fold_in(key, 71)
    slow_key, rate_key, residue_key = jax.random.split(base_key, 3)
    slow_share = 0.5
    slow_flag = jax.random.uniform(slow_key, (GROUPS, 1)) < slow_share
    unit_draw = jax.random.uniform(rate_key, (GROUPS, MODES))
    slow_rates = jnp.exp(jnp.log(0.2 / SEQ) + unit_draw * jnp.log(10.0))
    fast_rates = jnp.exp(jnp.log(1.0 / 50.0) + unit_draw * jnp.log(50.0 / 30.0))
    rate_values = jnp.where(slow_flag, slow_rates, fast_rates)
    residue_values = jnp.clip(jax.random.normal(residue_key, (GROUPS, MODES)), -6.0, 6.0) * jnp.sqrt(2.0 * rate_values / MODES)
    return (rate_values.astype(jnp.float32), residue_values.astype(jnp.float32))


def draw_decay_rates(key, part):
    return decay_pair(key)[0]


def draw_residues(key, part):
    return decay_pair(key)[1]


def draw_lengths(key, part):
    first_key, second_key = jax.random.split(jax.random.fold_in(key, 5))
    drawn = jax.random.randint(first_key, (SAMPLES,), SEQ // 2, SEQ + 1)
    chosen = jax.random.randint(second_key, (), 0, SAMPLES)
    return jnp.where(jnp.arange(SAMPLES) == chosen, SEQ, drawn).astype(jnp.int32)


def draw_query_act(key, part):
    base_key = jax.random.fold_in(jax.random.fold_in(key, 13), 0)
    channel_ramp = 0.6 + 1.2 * jnp.arange(D).astype(jnp.float32) / D
    values = jnp.clip(jax.random.normal(base_key, (SAMPLES, SEQ, D)), -6.0, 6.0)
    return (values * channel_ramp).astype(jnp.bfloat16)


def touch_ends(result, stream_key, smallest, high):
    place = [jax.random.randint(jax.random.fold_in(stream_key, axis), (), 0, length) for axis, length in enumerate(result.shape)]
    longest = result.shape.index(max(result.shape))
    neighbour = place[:longest] + [(place[longest] + 1) % result.shape[longest]] + place[longest + 1:]
    return result.at[tuple(place)].set(smallest).at[tuple(neighbour)].set(high)


def block_scale(own_key, extent, cuts, low, largest):
    factor_of, own = 1.0, jax.random.fold_in(own_key, 6)
    for dim, blocks in cuts:
        draws = jnp.exp(jax.random.uniform(jax.random.fold_in(own, dim), (blocks,), jnp.float32, low / len(cuts), largest / len(cuts)))
        factor_of = factor_of * jnp.repeat(draws, extent[dim] // blocks).reshape([-1 if axis == dim else 1 for axis in range(len(extent))])
    return factor_of


def rank_table(count, skew):
    weights = [(1 << 20) // math.isqrt(rank ** skew) + 1 for rank in range(1, count + 1)]
    width = 1 + sum(weights) // (1 << 30)
    return np.cumsum(np.array([max(1, weight // width) for weight in weights]))


def skewed_ids(own_key, extent, count, slope):
    listing = rank_table(count, slope)
    pick = jax.random.randint(jax.random.fold_in(own_key, 1), extent, 0, int(listing[count - 1]))
    standing = jnp.searchsorted(jnp.asarray(listing, jnp.int32), pick, side="right")
    return jax.random.permutation(jax.random.fold_in(own_key, 2), count)[standing].astype(jnp.int32)


def gaussian(own_key, extent, deviation, reach, cuts=(), held_as=jnp.bfloat16):
    entries = jax.random.normal(own_key, extent, jnp.float32) * deviation
    if len(cuts) > 0:
        entries = block_scale(own_key, extent, cuts, -0.22, 0.18) * entries
    return jnp.clip(entries, min=-reach, max=reach).astype(held_as)


def setup_inputs(seed: int = 0) -> dict:
    key_list = jax.random.split(jax.random.key(seed), 12)
    return {
        "token_ids": touch_ends(skewed_ids(key_list[0], (SAMPLES, SEQ), V, 2), jax.random.fold_in(key_list[0], 3), 0, V - 1).astype(jnp.int32),
        "lengths": draw_lengths(jax.random.fold_in(key_list[11], 71), 0),
        "embedding": gaussian(key_list[2], (V, D), 1.0, 6.0, ((1, 16),)),
        "query_act": draw_query_act(jax.random.fold_in(key_list[11], 71), 0),
        "key_act": gaussian(key_list[4], (SAMPLES, SEQ, D), 1.0, 6.0, ((1, 32), (2, 16))),
        "value_act": gaussian(key_list[5], (SAMPLES, SEQ, D), 1.0, 6.0, ((1, 32), (2, 16))),
        "short_filter": gaussian(key_list[6], (GROUPS, TAPS), TAPS ** -0.5, 0.5, ((0, 16),)),
        "decay_rates": draw_decay_rates(jax.random.fold_in(key_list[11], 71), 0),
        "residues": draw_residues(jax.random.fold_in(key_list[11], 71), 0),
        "skip_gain": jnp.clip(0.5 + 1.0 * jax.random.uniform(key_list[9], (D,), jnp.float32) ** block_scale(key_list[9], (D,), ((0, 16),), -0.2, 0.2), 0.5, 1.5),
        "norm_gain": jnp.clip(1.0 + 0.15 * jax.random.normal(key_list[10], (D,), jnp.float32), 0.25, 1.75),
    }


def causal_conv(signal, kernel):
    length = signal.shape[1]
    spectrum = jnp.fft.rfft(signal, n=2 * length, axis=1) * jnp.fft.rfft(kernel, n=2 * length, axis=0)[None]
    return jnp.fft.irfft(spectrum, n=2 * length, axis=1)[:, :length]

def reference(token_ids, lengths, embedding, query_act, key_act, value_act, short_filter, decay_rates, residues, skip_gain, norm_gain):
    block_width = 32 * GROUP
    block_count = D // block_width
    positions = jnp.arange(SEQ).astype(jnp.float32)

    def one_block(block_index):
        first_col = (block_index * block_width).astype(jnp.int32)
        first_group = (block_index * 32).astype(jnp.int32)
        gate_part = lax.dynamic_slice_in_dim(query_act, first_col, block_width, 2).astype(jnp.float32)
        key_part = lax.dynamic_slice_in_dim(key_act, first_col, block_width, 2).astype(jnp.float32)
        value_part = lax.dynamic_slice_in_dim(value_act, first_col, block_width, 2).astype(jnp.float32)
        product = lax.optimization_barrier((key_part * value_part).astype(jnp.bfloat16)).astype(jnp.float32)
        taps_part = lax.dynamic_slice_in_dim(short_filter, first_group, 32, 0).astype(jnp.float32)
        short_kernel = jnp.repeat(taps_part, GROUP, axis=0).T
        mixed = causal_conv(product, short_kernel)
        mixed = lax.optimization_barrier(mixed.astype(jnp.bfloat16)).astype(jnp.float32)
        rate_part = lax.dynamic_slice_in_dim(decay_rates, first_group, 32, 0)
        residue_part = lax.dynamic_slice_in_dim(residues, first_group, 32, 0)
        long_kernel = lax.optimization_barrier(jnp.sum(residue_part[:, :, None] * jnp.exp(-rate_part[:, :, None] * positions[None, None, :]), axis=1))
        filtered = causal_conv(mixed, jnp.repeat(long_kernel, GROUP, axis=0).T)
        filtered = lax.optimization_barrier(filtered.astype(jnp.bfloat16)).astype(jnp.float32)
        skip_part = lax.dynamic_slice_in_dim(skip_gain, first_col, block_width, 0)
        return gate_part * (filtered + skip_part * mixed)
    pieces = lax.map(one_block, jnp.arange(block_count).astype(jnp.int32))
    gated = jnp.moveaxis(pieces, 0, 2).reshape(SAMPLES, SEQ, D)
    mean_square = lax.optimization_barrier(jnp.sum(gated * gated, axis=2, keepdims=True)) / D
    normed = gated * lax.rsqrt(mean_square + 1e-06) * norm_gain
    embedded = jnp.take(embedding, token_ids, axis=0).astype(jnp.float32)
    valid = jnp.arange(SEQ)[None, :] < lengths[:, None]
    return jnp.where(valid[:, :, None], embedded + normed, 0.0).astype(jnp.bfloat16)
```

```python
import jax
import jax.numpy as jnp
from jax import lax
from jax.experimental import pallas as pl
from jax.experimental.pallas import tpu as pltpu
from jax.sharding import PartitionSpec as P

GROUP = 16
LANES = 128
TILE_GROUPS = LANES // GROUP
F32 = jnp.float32
BF16 = jnp.bfloat16


def iota(shape, dim, dtype=jnp.int32):
    return lax.broadcasted_iota(jnp.int32, shape, dim).astype(dtype)


def column(values):
    groups, modes = values.shape
    spread = jnp.broadcast_to(values[:, None, :], (groups, modes, modes))
    same = iota(spread.shape, 1) == iota(spread.shape, 2)
    picked = jnp.sum(jnp.where(same, spread, 0.0), axis=2, keepdims=True)
    return picked.reshape(groups * modes, 1)


def own_group(stacked, rows):
    lane_group = iota((rows, LANES), 1) // GROUP
    picked = stacked[:rows]
    for g in range(1, TILE_GROUPS):
        picked = jnp.where(lane_group == g, stacked[g * rows : (g + 1) * rows], picked)
    return picked


def halves(values):
    upper = values.astype(BF16)
    return upper, (values - upper.astype(F32)).astype(BF16)


def dot(a, b):
    return jnp.dot(a, b, preferred_element_type=F32)


def states_kernel(key_ref, value_ref, rate_ref, product_ref, state_ref, border_ref):
    samples, rows, _ = key_ref.shape
    taps = 128
    modes = rate_ref.shape[1]
    rate = column(rate_ref[...])
    weights = jnp.exp(-rate * (rows - 1.0 - iota((1, rows), 1, F32)))
    weights = jnp.concatenate(halves(weights), axis=0)
    half = weights.shape[0] // 2
    for s in range(samples):
        product = (key_ref[s].astype(F32) * value_ref[s].astype(F32)).astype(BF16)
        product_ref[s] = product
        full = dot(weights, product)
        state_ref[s * modes : (s + 1) * modes, :] = own_group(full[:half] + full[half:], modes)
        early = dot(weights[:, taps:], product[: rows - taps])
        upper, lower = halves(own_group(early[:half] + early[half:], modes))
        border_ref[s * taps : (s + 1) * taps, :] = product[rows - taps :]
        first = samples * taps + s * modes
        border_ref[first : first + modes, :] = upper
        border_ref[first + samples * modes : first + (samples + 1) * modes, :] = lower


def scan_kernel(first_ref, rate_ref, state_ref, out_ref, *, chunks, rows):
    total, width = state_ref.shape
    each = total // chunks
    groups, modes = rate_ref.shape
    rates = rate_ref[...]
    for r in range(each):
        mode = lax.rem(first_ref[0] * each + r, modes)
        picked = jnp.sum(
            jnp.where(iota(rates.shape, 1) == mode, rates, 0.0), axis=1, keepdims=True
        )
        at_group = iota((groups, width), 0) == iota((groups, width), 1) // GROUP
        rate = jnp.sum(jnp.where(at_group, picked, 0.0), axis=0, keepdims=True)
        decay = jnp.exp(-rate * float(rows))
        held = jnp.zeros((1, width), F32)
        out_ref[r : r + 1, :] = held
        for n in range(1, chunks):
            out_ref[n * each + r : n * each + r + 1, :] = held
            held = decay * held + state_ref[(n - 1) * each + r : (n - 1) * each + r + 1, :]


def local_kernel(
    product_ref,
    border_ref,
    filter_ref,
    rate_ref,
    residue_ref,
    mixed_ref,
    local_ref,
    upper_ref,
    lower_ref,
    factor_ref,
    short_table,
    long_table,
    product_window,
    mixed_window,
):
    samples, rows, _ = product_ref.shape
    modes = rate_ref.shape[1]
    taps = 128
    span = rows + taps
    blocks = rows // taps
    rate = column(rate_ref[...])
    residue = column(residue_ref[...])
    filters = filter_ref[...]

    reverse = (iota((taps, 2 * taps), 0) + iota((taps, 2 * taps), 1) == taps).astype(BF16)
    short_base = dot(filters, reverse)
    wide = span + taps
    place = iota((1, wide), 1)
    lag = jnp.where(place <= rows, rows - place, rows + wide - place)
    zero = jnp.logical_and(place > rows, place <= rows + taps)
    modal = residue * jnp.exp(-rate * lag.astype(F32))
    modal = jnp.where(zero, 0.0, modal)
    long_base = jnp.sum(modal.reshape(TILE_GROUPS, modes, wide), axis=1)
    for g in range(TILE_GROUPS):
        spread = jnp.broadcast_to(short_base[g : g + 1], (taps, 2 * taps))
        rolled = pltpu.roll(spread, 0, 1, stride=1, stride_axis=0)
        short_table[g * taps : (g + 1) * taps, :] = rolled.astype(BF16)
        spread = jnp.broadcast_to(long_base[g : g + 1], (taps, wide))
        rolled = pltpu.roll(spread, 0, 1, stride=1, stride_axis=0)
        long_table[g * taps : (g + 1) * taps, :] = rolled[:, :span].astype(BF16)

    for s in range(samples):
        product_window[s, 0:taps, :] = jnp.zeros((taps, LANES), BF16)
        product_window[s, taps : 2 * taps, :] = border_ref[s * taps : (s + 1) * taps, :]
        product_window[s, 2 * taps :, :] = product_ref[s]

    def short_step(step, _):
        s = step // (blocks + 1)
        first = pl.multiple_of(lax.rem(step, blocks + 1) * taps, taps)
        full = dot(short_table[...], product_window[s, pl.ds(first, 2 * taps), :])
        mixed_window[s, pl.ds(first, taps), :] = own_group(full, taps).astype(BF16)
        return _

    lax.fori_loop(0, samples * (blocks + 1), short_step, 0)

    def long_step(s, _):
        mixed_ref[s] = mixed_window[s, taps:, :]
        for b in range(1, blocks + 1):
            full = dot(long_table[:, (blocks - b) * taps :], mixed_window[s, : (b + 1) * taps, :])
            local_ref[s, (b - 1) * taps : b * taps, :] = own_group(full, taps)
        return _

    lax.fori_loop(0, samples, long_step, 0)

    after = jnp.exp(-rate * (1.0 + iota((1, rows), 1, F32)))
    upper, lower = halves(after.T)
    upper_ref[...] = upper
    lower_ref[...] = lower
    tap_weights = jnp.exp(-rate * (taps - iota((1, taps), 1, F32)))
    spread = jnp.broadcast_to(
        filters.astype(F32)[:, None, :], (TILE_GROUPS, modes, taps)
    ).reshape(TILE_GROUPS * modes, taps)
    gain = residue * jnp.sum(spread * tap_weights, axis=1, keepdims=True)
    square = (TILE_GROUPS * modes, LANES)
    factor_ref[:modes, :] = own_group(
        jnp.broadcast_to(jnp.exp(-rate * float(rows - taps)), square), modes
    )
    factor_ref[modes:, :] = own_group(jnp.broadcast_to(gain, square), modes)


def embed_kernel(token_ref, table_ref, out_ref):
    samples, rows = token_ref.shape
    vocab = table_ref.shape[0]
    for s in range(samples):
        ids = jnp.broadcast_to(token_ref[s : s + 1, :].astype(F32), (8, rows)).T[:, :1]
        one_hot = (ids == iota((rows, vocab), 1, F32)).astype(BF16)
        out_ref[s] = dot(one_hot, table_ref[...]).astype(BF16)


def gate_kernel(
    carried_ref,
    early_ref,
    factor_ref,
    upper_ref,
    lower_ref,
    local_ref,
    mixed_ref,
    query_ref,
    skip_ref,
    gated_ref,
    sum_ref,
    squares,
):
    samples, rows, _ = local_ref.shape
    modes = factor_ref.shape[0] // 2
    copies = sum_ref.shape[0]
    step = pl.program_id(0)
    own = iota((LANES, LANES), 0) // modes == iota((LANES, LANES), 1) // GROUP
    early = early_ref[...].astype(F32)
    early = early[: samples * modes] + early[samples * modes :]
    skip = skip_ref[...]
    for s in range(samples):
        part = slice(s * modes, (s + 1) * modes)
        state = factor_ref[:modes, :] * carried_ref[part, :] + early[part]
        state = state * factor_ref[modes:, :]
        spread = jnp.concatenate([state] * TILE_GROUPS, axis=0)
        upper, lower = halves(jnp.where(own, spread, 0.0))
        carry = (
            dot(upper_ref[...], upper) + dot(upper_ref[...], lower) + dot(lower_ref[...], upper)
        )
        filtered = (local_ref[s] + carry).astype(BF16).astype(F32)
        gated = query_ref[s].astype(F32) * (filtered + skip * mixed_ref[s].astype(F32))
        gated_ref[s] = gated
        square = gated * gated

        @pl.when(step == 0)
        def _():
            squares[s] = square

        @pl.when(step > 0)
        def _():
            squares[s] = squares[s] + square

    @pl.when(step == pl.num_programs(0) - 1)
    def _():
        for s in range(samples):
            total = jnp.sum(squares[s].T, axis=0, keepdims=True)
            sum_ref[:, s * rows : (s + 1) * rows] = jnp.broadcast_to(total, (copies, rows))


def norm_kernel(length_ref, index_ref, sum_ref, gated_ref, embed_ref, gain_ref, out_ref, *, full, rows):
    _, here, _ = gated_ref.shape
    s = pl.program_id(0)
    total = jnp.sum(sum_ref[...], axis=0, keepdims=True)
    scale = lax.rsqrt(total / full + 1e-06)
    scale = jnp.broadcast_to(scale, (8, here)).T[:, :1]
    start = index_ref[0] * rows + pl.program_id(1) * here
    valid = start + iota((here, 1), 0) < length_ref[s]
    value = gated_ref[0] * scale * gain_ref[...] + embed_ref[0].astype(F32)
    out_ref[0] = jnp.where(valid, value, 0.0).astype(BF16)


def params(mebibytes):
    return pltpu.CompilerParams(vmem_limit_bytes=mebibytes << 20)


def per_device(
    token_ids,
    lengths,
    embedding,
    query_act,
    key_act,
    value_act,
    short_filter,
    decay_rates,
    residues,
    skip_gain,
    norm_gain,
):
    samples, rows, width = query_act.shape
    taps = short_filter.shape[1]
    groups, modes = decay_rates.shape
    vocab = embedding.shape[0]
    chunks = lax.axis_size("ctx")
    columns = lax.axis_size("tp")
    index = lax.axis_index("ctx").reshape(1)
    tiles = width // LANES
    smem = pl.BlockSpec(memory_space=pltpu.SMEM)

    def cube():
        return pl.BlockSpec((samples, rows, LANES), lambda i: (0, 0, i))

    def flat(height):
        return pl.BlockSpec((height, LANES), lambda i: (0, i))

    def grouped(cols):
        return pl.BlockSpec((TILE_GROUPS, cols), lambda i: (i, 0))

    state_rows = samples * modes
    border_rows = samples * taps + 2 * state_rows
    shape = jax.ShapeDtypeStruct

    product, states, border = pl.pallas_call(
        states_kernel,
        grid=(tiles,),
        in_specs=[cube(), cube(), grouped(modes)],
        out_specs=[cube(), flat(state_rows), flat(border_rows)],
        out_shape=[
            shape((samples, rows, width), BF16),
            shape((state_rows, width), F32),
            shape((border_rows, width), BF16),
        ],
        compiler_params=params(16),
        name="states",
    )(key_act, value_act, decay_rates)

    gathered = lax.all_to_all(states, "ctx", split_axis=0, concat_axis=0, tiled=True)
    before = lax.ppermute(border, "ctx", [(i, i + 1) for i in range(chunks - 1)])

    embedded = pl.pallas_call(
        embed_kernel,
        out_shape=shape((samples, rows, width), BF16),
        cost_estimate=pl.CostEstimate(
            flops=2 * samples * rows * width * vocab, bytes_accessed=4 << 20, transcendentals=0
        ),
        compiler_params=params(16),
        name="embed",
    )(token_ids, embedding)

    mixed, local, upper, lower, factors = pl.pallas_call(
        local_kernel,
        grid=(tiles,),
        in_specs=[cube(), flat(border_rows), grouped(taps), grouped(modes), grouped(modes)],
        out_specs=[cube(), cube(), flat(rows), flat(rows), flat(2 * modes)],
        out_shape=[
            shape((samples, rows, width), BF16),
            shape((samples, rows, width), F32),
            shape((rows, width), BF16),
            shape((rows, width), BF16),
            shape((2 * modes, width), F32),
        ],
        scratch_shapes=[
            pltpu.VMEM((TILE_GROUPS * taps, 2 * taps), BF16),
            pltpu.VMEM((TILE_GROUPS * taps, rows + taps), BF16),
            pltpu.VMEM((samples, rows + 2 * taps, LANES), BF16),
            pltpu.VMEM((samples, rows + taps, LANES), BF16),
        ],
        cost_estimate=pl.CostEstimate(
            flops=12_000_000_000, bytes_accessed=8 << 20, transcendentals=1 << 20
        ),
        compiler_params=params(32),
        name="local",
    )(product, before, short_filter, decay_rates, residues)

    def scan(first_ref, rate_ref, state_ref, out_ref):
        scan_kernel(first_ref, rate_ref, state_ref, out_ref, chunks=chunks, rows=rows)

    entering = pl.pallas_call(
        scan,
        in_specs=[smem, pl.BlockSpec(), pl.BlockSpec()],
        out_shape=shape((state_rows, width), F32),
        compiler_params=params(8),
        name="scan",
    )(index, decay_rates, gathered)
    carried = lax.all_to_all(entering, "ctx", split_axis=0, concat_axis=0, tiled=True)

    early_at = samples * taps // (2 * state_rows)
    gated, sums = pl.pallas_call(
        gate_kernel,
        grid=(tiles,),
        in_specs=[
            flat(state_rows),
            pl.BlockSpec((2 * state_rows, LANES), lambda i: (early_at, i)),
            flat(2 * modes),
            flat(rows),
            flat(rows),
            cube(),
            cube(),
            cube(),
            flat(1),
        ],
        out_specs=[cube(), pl.BlockSpec((columns, samples * rows), lambda i: (0, 0))],
        out_shape=[shape((samples, rows, width), F32), shape((columns, samples * rows), F32)],
        scratch_shapes=[pltpu.VMEM((samples, rows, LANES), F32)],
        compiler_params=params(16),
        name="gate",
    )(
        carried,
        before,
        factors,
        upper,
        lower,
        local,
        mixed,
        query_act,
        skip_gain.reshape(1, width),
    )
    shares = lax.all_to_all(sums, "tp", split_axis=0, concat_axis=0, tiled=True)

    parts = 2
    here = rows // parts

    def norm(length_ref, index_ref, sum_ref, gated_ref, embed_ref, gain_ref, out_ref):
        norm_kernel(
            length_ref,
            index_ref,
            sum_ref,
            gated_ref,
            embed_ref,
            gain_ref,
            out_ref,
            full=float(columns * width),
            rows=rows,
        )

    block = pl.BlockSpec((1, here, width), lambda s, i: (s, i, 0))
    return pl.pallas_call(
        norm,
        grid=(samples, parts),
        in_specs=[
            smem,
            smem,
            pl.BlockSpec((columns, here), lambda s, i: (0, s * parts + i)),
            block,
            block,
            pl.BlockSpec((1, width), lambda s, i: (0, 0)),
        ],
        out_specs=block,
        out_shape=shape((samples, rows, width), BF16),
        compiler_params=params(16),
        name="norm",
    )(lengths, index, shares, gated, embedded, norm_gain.reshape(1, width))


def solution(mesh):
    placed = (
        P(None, "ctx"),
        P(),
        P(None, "tp"),
        P(None, "ctx", "tp"),
        P(None, "ctx", "tp"),
        P(None, "ctx", "tp"),
        P("tp", None),
        P("tp", None),
        P("tp", None),
        P("tp"),
        P("tp"),
    )
    return jax.shard_map(
        per_device, mesh=mesh, in_specs=placed, out_specs=P(None, "ctx", "tp"), check_vma=False
    )
```

```python
import jax
import jax.numpy as jnp
from jax import lax
from jax.experimental import pallas as pl
from jax.experimental.pallas import tpu as pltpu
from jax.sharding import PartitionSpec as P

GROUP = 16
LANES = 128
TILE_GROUPS = LANES // GROUP
F32 = jnp.float32
BF16 = jnp.bfloat16


def iota(shape, dim, dtype=jnp.int32):
    return lax.broadcasted_iota(jnp.int32, shape, dim).astype(dtype)


def own_group(stacked, rows):
    lane_group = iota((rows, LANES), 1) // GROUP
    picked = stacked[:rows]
    for g in range(1, TILE_GROUPS):
        picked = jnp.where(lane_group == g, stacked[g * rows : (g + 1) * rows], picked)
    return picked


def halves(values):
    upper = values.astype(BF16)
    return upper, (values - upper.astype(F32)).astype(BF16)


def dot(a, b):
    return jnp.dot(a, b, preferred_element_type=F32)


def tile_column(table, tile):
    modes, groups = table.shape
    parts = []
    for g in range(TILE_GROUPS):
        here = iota((modes, groups), 1) == tile * TILE_GROUPS + g
        parts.append(jnp.sum(jnp.where(here, table, 0.0), axis=1, keepdims=True))
    return jnp.concatenate(parts, axis=0)


def product_of(key_ref, value_ref, s):
    return (key_ref[s].astype(F32) * value_ref[s].astype(F32)).astype(BF16)


def states_kernel(rate_ref, key_ref, value_ref, state_ref, *, rows):
    samples, here, width = key_ref.shape
    modes = rate_ref.shape[0]
    step = pl.program_id(0)
    first = (rows - 1 - step * here).astype(F32)
    lag = first - iota((1, here), 1, F32)
    for tile in range(width // LANES):
        lanes = slice(tile * LANES, (tile + 1) * LANES)
        weights = jnp.exp(-tile_column(rate_ref[...], tile) * lag)
        weights = jnp.concatenate(halves(weights), axis=0)
        half = weights.shape[0] // 2
        for s in range(samples):
            key, value = key_ref[s, :, lanes].astype(F32), value_ref[s, :, lanes].astype(F32)
            full = dot(weights, (key * value).astype(BF16))
            state = own_group(full[:half] + full[half:], modes).reshape(modes, 1, LANES)
            part = slice(s * modes, (s + 1) * modes)

            @pl.when(step == 0)
            def _():
                state_ref[part, :, lanes] = state

            @pl.when(step > 0)
            def _():
                state_ref[part, :, lanes] = state_ref[part, :, lanes] + state


def border_kernel(rate_ref, key_ref, value_ref, border_ref, *, taps):
    samples, rows, _ = key_ref.shape
    modes = rate_ref.shape[0]
    early = rows - taps
    rate = tile_column(rate_ref[...], pl.program_id(0))
    weights = jnp.exp(-rate * (early - 1.0 - iota((1, early), 1, F32)))
    weights = jnp.concatenate(halves(weights), axis=0)
    half = weights.shape[0] // 2
    for s in range(samples):
        product = product_of(key_ref, value_ref, s)
        border_ref[s * taps : (s + 1) * taps, :] = product[early:]
        full = dot(weights, product[:early])
        upper, lower = halves(own_group(full[:half] + full[half:], modes))
        first = samples * taps + s * modes
        border_ref[first : first + modes, :] = upper
        border_ref[first + samples * modes : first + (samples + 1) * modes, :] = lower


def early_kernel(border_ref, out_ref, mark_ref):
    mark_ref[...] = jnp.zeros_like(mark_ref)
    height = out_ref.shape[0]
    upper = border_ref[:height, :].astype(F32)
    out_ref[...] = upper + border_ref[height:, :].astype(F32)


def scan_kernel(first_ref, rate_ref, state_ref, out_ref, *, chunks, rows):
    total, _, width = state_ref.shape
    each = total // chunks
    groups, modes = rate_ref.shape
    rates = rate_ref[...]
    for r in range(each):
        mode = lax.rem(first_ref[0] * each + r, modes)
        picked = jnp.sum(
            jnp.where(iota(rates.shape, 1) == mode, rates, 0.0), axis=1, keepdims=True
        )
        at_group = iota((groups, width), 0) == iota((groups, width), 1) // GROUP
        rate = jnp.sum(jnp.where(at_group, picked, 0.0), axis=0, keepdims=True)
        decay = jnp.exp(-rate * float(rows))
        held = jnp.zeros((1, width), F32)
        out_ref[r] = held
        for n in range(1, chunks):
            out_ref[n * each + r] = held
            held = decay * held + state_ref[(n - 1) * each + r]


def dot_rows(a, b):
    return lax.dot_general(a, b, (((1,), (1,)), ((), ())), preferred_element_type=F32)


def local_kernel(
    border_ref,
    key_ref,
    value_ref,
    filter_ref,
    rate_ref,
    residue_ref,
    skip_ref,
    base_ref,
    factor_ref,
    product_window,
    mixed_window,
    turned,
):
    samples, rows, _ = key_ref.shape
    modes = rate_ref.shape[0]
    taps = filter_ref.shape[1]
    span = rows + taps
    blocks = rows // taps
    before = span - 2 * taps
    tile = pl.program_id(0)
    rate = tile_column(rate_ref[...], tile)
    residue = tile_column(residue_ref[...], tile)
    filters = filter_ref[...]

    reverse = (iota((taps, 2 * taps), 0) + iota((taps, 2 * taps), 1) == taps).astype(BF16)
    short_base = dot(filters, reverse)
    wide = span + taps
    place = iota((1, wide), 1)
    lag = jnp.where(place <= rows, rows - place, rows + wide - place)
    zero = jnp.logical_and(place > rows, place <= span)
    modal = residue * jnp.exp(-rate * lag.astype(F32))
    modal = jnp.where(zero, 0.0, modal)
    long_base = jnp.sum(modal.reshape(TILE_GROUPS, modes, wide), axis=1)

    for s in range(samples):
        product_window[s, :, :taps] = jnp.zeros((LANES, taps), BF16)
        mixed_window[s, :, :before] = jnp.zeros((LANES, before), BF16)
        border = border_ref[s * taps : (s + 1) * taps, :].astype(F32)
        product_window[s, :, taps : 2 * taps] = border.T.astype(BF16)
        product = product_of(key_ref, value_ref, s).astype(F32)
        product_window[s, :, 2 * taps :] = product.T.astype(BF16)

    skip = jnp.broadcast_to(skip_ref[...], (8, LANES)).T[:, :1]
    for g in range(TILE_GROUPS):
        channels = slice(g * GROUP, (g + 1) * GROUP)
        spread = jnp.broadcast_to(short_base[g : g + 1], (taps, 2 * taps))
        short_table = pltpu.roll(spread, 0, 1, stride=1, stride_axis=0).astype(BF16)
        pieces = [
            product_window[s, channels, b * taps : (b + 2) * taps]
            for s in range(samples)
            for b in range(blocks + 1)
        ]
        mixed = dot_rows(jnp.concatenate(pieces, axis=0), short_table).astype(BF16)
        for s in range(samples):
            for b in range(blocks + 1):
                first = (s * (blocks + 1) + b) * GROUP
                mixed_window[s, channels, before + b * taps : before + (b + 1) * taps] = mixed[
                    first : first + GROUP
                ]
        spread = jnp.broadcast_to(long_base[g : g + 1], (taps, wide))
        long_table = pltpu.roll(spread, 0, 1, stride=1, stride_axis=0)[:, :span].astype(BF16)
        pieces = [
            mixed_window[s, channels, b * taps : b * taps + span]
            for s in range(samples)
            for b in range(blocks)
        ]
        filtered = dot_rows(jnp.concatenate(pieces, axis=0), long_table)
        for s in range(samples):
            for b in range(blocks):
                first = (s * blocks + b) * GROUP
                at = (s * (blocks + 1) + b + 1) * GROUP
                turned[s, channels, b * taps : (b + 1) * taps] = filtered[
                    first : first + GROUP
                ] + skip[channels] * mixed[at : at + GROUP].astype(F32)
    for s in range(samples):
        base_ref[s] = turned[s].T.astype(BF16)

    tap_weights = jnp.exp(-rate * (taps - iota((1, taps), 1, F32)))
    spread = jnp.broadcast_to(
        filters.astype(F32)[:, None, :], (TILE_GROUPS, modes, taps)
    ).reshape(TILE_GROUPS * modes, taps)
    gain = residue * jnp.sum(spread * tap_weights, axis=1, keepdims=True)
    square = (TILE_GROUPS * modes, LANES)
    factor_ref[:modes, :] = own_group(
        jnp.broadcast_to(jnp.exp(-rate * float(rows - taps)), square), modes
    )
    factor_ref[modes:, :] = own_group(jnp.broadcast_to(gain, square), modes)


def embed_kernel(token_ref, table_ref, out_ref, mark_ref):
    mark_ref[...] = jnp.zeros_like(mark_ref)
    samples, rows = token_ref.shape
    vocab = table_ref.shape[0]
    for s in range(samples):
        ids = jnp.broadcast_to(token_ref[s : s + 1, :].astype(F32), (8, rows)).T[:, :1]
        one_hot = (ids == iota((rows, vocab), 1, F32)).astype(BF16)
        out_ref[s] = dot(one_hot, table_ref[...]).astype(BF16)


def gate_kernel(
    carried_ref,
    early_ref,
    factor_ref,
    rate_ref,
    base_source,
    query_source,
    gated_ref,
    sum_ref,
    base_ref,
    query_ref,
    squares,
    arrived,
):
    samples, rows, width = base_ref.shape
    modes = factor_ref.shape[0] // 2
    copies = sum_ref.shape[0]
    own = iota((LANES, LANES), 0) // modes == iota((LANES, LANES), 1) // GROUP
    tiles = [slice(first, first + LANES) for first in range(0, width, LANES)]
    loads = []
    for tile, lanes in enumerate(tiles):
        pair = (
            pltpu.make_async_copy(
                base_source.at[:, :, lanes], base_ref.at[:, :, lanes], arrived.at[0, tile]
            ),
            pltpu.make_async_copy(
                query_source.at[:, :, lanes], query_ref.at[:, :, lanes], arrived.at[1, tile]
            ),
        )
        for load in pair:
            load.start()
        loads.append(pair)
    for tile, lanes in enumerate(tiles):
        rate = rate_ref[:, lanes]
        head = jnp.exp(-rate * (1.0 + iota((LANES, 1), 0, F32)))
        step = jnp.exp(-rate * float(LANES))
        after = [head]
        for _ in range(rows // LANES - 1):
            after.append(after[-1] * step)
        upper, lower = halves(jnp.concatenate(after, axis=0))
        after = jnp.concatenate([upper, lower, upper], axis=1)
        for load in loads[tile]:
            load.wait()
        for s in range(samples):
            part = slice(s * modes, (s + 1) * modes)
            carried = carried_ref[part, :, lanes].reshape(modes, LANES)
            state = factor_ref[:modes, lanes] * carried + early_ref[part, lanes]
            state = state * factor_ref[modes:, lanes]
            spread = jnp.concatenate([state] * TILE_GROUPS, axis=0)
            upper, lower = halves(jnp.where(own, spread, 0.0))
            carry = dot(after, jnp.concatenate([upper, upper, lower], axis=0))
            base = base_ref[s, :, lanes].astype(F32)
            gated = query_ref[s, :, lanes].astype(F32) * (base + carry)
            gated_ref[s, :, lanes] = gated
            if tile == 0:
                squares[s] = gated * gated
            else:
                squares[s] = squares[s] + gated * gated
    for s in range(samples):
        total = jnp.sum(squares[s].T, axis=0, keepdims=True)
        sum_ref[:, :, s * rows : (s + 1) * rows] = jnp.broadcast_to(
            total.reshape(1, 1, rows), (copies, 1, rows)
        )


def norm_kernel(
    length_ref, index_ref, sum_ref, gated_ref, embed_ref, gain_ref, out_target, out_ref, left, *, full
):
    samples, rows, _ = gated_ref.shape
    here = 128
    total = jnp.sum(sum_ref[...], axis=0)
    scale = jnp.broadcast_to(lax.rsqrt(total / full + 1e-06), (8, samples * rows)).T[:, :1]
    stores = []
    for s in range(samples):
        for part in range(rows // here):
            at = slice(part * here, (part + 1) * here)
            start = index_ref[0] * rows + part * here
            valid = start + iota((here, 1), 0) < length_ref[s]
            first = s * rows + part * here
            value = gated_ref[s, at, :] * scale[first : first + here] * gain_ref[...]
            value = value + embed_ref[s, at, :].astype(F32)
            out_ref[s, at, :] = jnp.where(valid, value, 0.0).astype(BF16)
            store = pltpu.make_async_copy(
                out_ref.at[s, at, :], out_target.at[s, at, :], left.at[s, part]
            )
            store.start()
            stores.append(store)
    for store in stores:
        store.wait()


def params(mebibytes):
    return pltpu.CompilerParams(vmem_limit_bytes=mebibytes << 20)


def per_device(
    token_ids,
    lengths,
    embedding,
    query_act,
    key_act,
    value_act,
    short_filter,
    decay_rates,
    residues,
    skip_gain,
    norm_gain,
):
    samples, rows, width = query_act.shape
    taps = short_filter.shape[1]
    groups, modes = decay_rates.shape
    vocab = embedding.shape[0]
    chunks = lax.axis_size("ctx")
    columns = lax.axis_size("tp")
    index = lax.axis_index("ctx").reshape(1)
    tiles = width // LANES
    smem = pl.BlockSpec(memory_space=pltpu.SMEM)

    def cube():
        return pl.BlockSpec((samples, rows, LANES), lambda i: (0, 0, i))

    def flat(height):
        return pl.BlockSpec((height, LANES), lambda i: (0, i))

    def grouped(cols):
        return pl.BlockSpec((TILE_GROUPS, cols), lambda i: (i, 0))

    state_rows = samples * modes
    border_rows = samples * taps + 2 * state_rows
    early_at = samples * taps // (2 * state_rows)
    shape = jax.ShapeDtypeStruct
    whole = pl.BlockSpec((modes, groups), lambda i: (0, 0))
    rates = decay_rates.T

    def states_step(rate_ref, key_ref, value_ref, state_ref):
        states_kernel(rate_ref, key_ref, value_ref, state_ref, rows=rows)

    slab = pl.BlockSpec((samples, rows // 2, width), lambda i: (0, i, 0))
    states = pl.pallas_call(
        states_step,
        grid=(2,),
        in_specs=[whole, slab, slab],
        out_specs=pl.BlockSpec((state_rows, 1, width), lambda i: (0, 0, 0)),
        out_shape=shape((state_rows, 1, width), F32),
        compiler_params=params(60),
        name="states",
    )(rates, key_act, value_act)
    gathered = lax.all_to_all(states, "ctx", split_axis=0, concat_axis=0, tiled=True)

    def border_step(rate_ref, key_ref, value_ref, border_ref):
        border_kernel(rate_ref, key_ref, value_ref, border_ref, taps=taps)

    key_late, value_late, _ = lax.optimization_barrier((key_act, value_act, states))
    border = pl.pallas_call(
        border_step,
        grid=(tiles,),
        in_specs=[whole, cube(), cube()],
        out_specs=flat(border_rows),
        out_shape=shape((border_rows, width), BF16),
        cost_estimate=pl.CostEstimate(
            flops=400_000_000, bytes_accessed=3 << 20, transcendentals=1 << 18
        ),
        compiler_params=params(60),
        name="border",
    )(rates, key_late, value_late)
    before = lax.ppermute(border, "ctx", [(i, i + 1) for i in range(chunks - 1)])

    early, early_mark = pl.pallas_call(
        early_kernel,
        grid=(1,),
        in_specs=[pl.BlockSpec((2 * state_rows, width), lambda i: (early_at, 0))],
        out_specs=[
            pl.BlockSpec((state_rows, width), lambda i: (0, 0)),
            pl.BlockSpec((8, LANES), lambda i: (0, 0)),
        ],
        out_shape=[shape((state_rows, width), F32), shape((8, LANES), F32)],
        compiler_params=params(60),
        name="early",
    )(before)

    embedded, embed_mark = pl.pallas_call(
        embed_kernel,
        out_shape=[shape((samples, rows, width), BF16), shape((8, LANES), F32)],
        cost_estimate=pl.CostEstimate(
            flops=40 * samples * rows * width * vocab, bytes_accessed=4 << 20, transcendentals=0
        ),
        compiler_params=params(16),
        name="embed",
    )(token_ids, embedding)

    base, factors = pl.pallas_call(
        local_kernel,
        grid=(tiles,),
        in_specs=[flat(border_rows), cube(), cube(), grouped(taps), whole, whole, flat(1)],
        out_specs=[cube(), flat(2 * modes)],
        out_shape=[
            shape((samples, rows, width), BF16),
            shape((2 * modes, width), F32),
        ],
        scratch_shapes=[
            pltpu.VMEM((samples, LANES, rows + 2 * taps), BF16),
            pltpu.VMEM((samples, LANES, 2 * rows), BF16),
            pltpu.VMEM((samples, LANES, rows), F32),
        ],
        cost_estimate=pl.CostEstimate(
            flops=12_000_000_000, bytes_accessed=8 << 20, transcendentals=1 << 20
        ),
        compiler_params=params(60),
        name="local",
    )(
        before,
        key_act,
        value_act,
        short_filter,
        rates,
        residues.T,
        skip_gain.reshape(1, width),
    )

    def scan(first_ref, rate_ref, state_ref, early_ref, embed_ref, out_ref):
        scan_kernel(first_ref, rate_ref, state_ref, out_ref, chunks=chunks, rows=rows)

    entering = pl.pallas_call(
        scan,
        in_specs=[smem, pl.BlockSpec(), pl.BlockSpec(), pl.BlockSpec(), pl.BlockSpec()],
        out_shape=shape((state_rows, 1, width), F32),
        compiler_params=params(8),
        name="scan",
    )(index, decay_rates, gathered, early_mark, embed_mark)
    carried = lax.all_to_all(entering, "ctx", split_axis=0, concat_axis=0, tiled=True)

    vmem = pl.BlockSpec(memory_space=pltpu.VMEM)
    anywhere = pl.BlockSpec(memory_space=pl.ANY)
    gated, sums = pl.pallas_call(
        gate_kernel,
        in_specs=[vmem, vmem, vmem, vmem, anywhere, anywhere],
        out_shape=[
            shape((samples, rows, width), F32),
            shape((columns, 1, samples * rows), F32),
        ],
        scratch_shapes=[
            pltpu.VMEM((samples, rows, width), BF16),
            pltpu.VMEM((samples, rows, width), BF16),
            pltpu.VMEM((samples, rows, LANES), F32),
            pltpu.SemaphoreType.DMA((2, tiles)),
        ],
        compiler_params=params(16),
        name="gate",
    )(carried, early, factors, decay_rates.reshape(1, groups * modes), base, query_act)
    shares = lax.all_to_all(sums, "tp", split_axis=0, concat_axis=0, tiled=True)

    def norm(*refs):
        norm_kernel(*refs, full=float(columns * width))

    return pl.pallas_call(
        norm,
        in_specs=[smem, smem, vmem, vmem, vmem, vmem],
        out_specs=anywhere,
        out_shape=shape((samples, rows, width), BF16),
        scratch_shapes=[
            pltpu.VMEM((samples, rows, width), BF16),
            pltpu.SemaphoreType.DMA((samples, rows // 128)),
        ],
        compiler_params=params(16),
        name="norm",
    )(lengths, index, shares, gated, embedded, norm_gain.reshape(1, width))


def solution(mesh):
    placed = (
        P(None, "ctx"),
        P(),
        P(None, "tp"),
        P(None, "ctx", "tp"),
        P(None, "ctx", "tp"),
        P(None, "ctx", "tp"),
        P("tp", None),
        P("tp", None),
        P("tp", None),
        P("tp"),
        P("tp"),
    )
    return jax.shard_map(
        per_device, mesh=mesh, in_specs=placed, out_specs=P(None, "ctx", "tp"), check_vma=False
    )
```

```python
import jax
import jax.numpy as jnp
from jax import lax
from jax.experimental import pallas as pl
from jax.experimental.pallas import tpu as pltpu
from jax.sharding import PartitionSpec as P

GROUP = 16
LANES = 128
TILE_GROUPS = LANES // GROUP
F32 = jnp.float32
BF16 = jnp.bfloat16


def iota(shape, dim, dtype=jnp.int32):
    return lax.broadcasted_iota(jnp.int32, shape, dim).astype(dtype)


def own_group(stacked, rows):
    lane_group = iota((rows, LANES), 1) // GROUP
    picked = stacked[:rows]
    for g in range(1, TILE_GROUPS):
        picked = jnp.where(lane_group == g, stacked[g * rows : (g + 1) * rows], picked)
    return picked


def halves(values):
    upper = values.astype(BF16)
    return upper, (values - upper.astype(F32)).astype(BF16)


def dot(a, b):
    return jnp.dot(a, b, preferred_element_type=F32)


def tile_column(table, tile):
    modes, groups = table.shape
    parts = []
    for g in range(TILE_GROUPS):
        here = iota((modes, groups), 1) == tile * TILE_GROUPS + g
        parts.append(jnp.sum(jnp.where(here, table, 0.0), axis=1, keepdims=True))
    return jnp.concatenate(parts, axis=0)


def product_of(key, value):
    return (key.astype(F32) * value.astype(F32)).astype(BF16)


def states_kernel(
    rate_ref, key_source, value_source, state_ref, border_ref, key_ref, value_ref, arrived, *, taps
):
    samples, rows, width = key_ref.shape
    modes = rate_ref.shape[0]
    tiles = [slice(first, first + LANES) for first in range(0, width, LANES)]
    loads = []
    for tile, lanes in enumerate(tiles):
        pair = (
            pltpu.make_async_copy(
                key_source.at[:, :, lanes], key_ref.at[:, :, lanes], arrived.at[0, tile]
            ),
            pltpu.make_async_copy(
                value_source.at[:, :, lanes], value_ref.at[:, :, lanes], arrived.at[1, tile]
            ),
        )
        for load in pair:
            load.start()
        loads.append(pair)
    for tile, lanes in enumerate(tiles):
        groups = range(tile * TILE_GROUPS, (tile + 1) * TILE_GROUPS)
        rate = jnp.concatenate([rate_ref[:, g : g + 1] for g in groups], axis=0)
        weights = [jnp.exp(-rate * (taps - 1.0 - iota((1, taps), 1, F32)))]
        step = jnp.exp(-rate * float(taps))
        for _ in range(rows // taps - 1):
            weights.insert(0, weights[0] * step)
        weights = jnp.concatenate(halves(jnp.concatenate(weights, axis=1)), axis=0)
        half = weights.shape[0] // 2
        for load in loads[tile]:
            load.wait()
        for s in range(samples):
            product = product_of(key_ref[s, :, lanes], value_ref[s, :, lanes])
            full = dot(weights, product)
            state = own_group(full[:half] + full[half:], modes)
            state_ref[s * modes : (s + 1) * modes, :, lanes] = state.reshape(modes, 1, LANES)
            border_ref[s * taps : (s + 1) * taps, lanes] = product[rows - taps :]
            early = dot(weights[:, taps:], product[: rows - taps])
            upper, lower = halves(own_group(early[:half] + early[half:], modes))
            first = samples * taps + s * modes
            border_ref[first : first + modes, lanes] = upper
            border_ref[first + samples * modes : first + (samples + 1) * modes, lanes] = lower


def scan_kernel(first_ref, rate_ref, state_ref, out_ref, *, chunks, rows):
    total, _, width = state_ref.shape
    each = total // chunks
    groups, modes = rate_ref.shape
    rates = rate_ref[...]
    for r in range(each):
        mode = lax.rem(first_ref[0] * each + r, modes)
        picked = jnp.sum(
            jnp.where(iota(rates.shape, 1) == mode, rates, 0.0), axis=1, keepdims=True
        )
        at_group = iota((groups, width), 0) == iota((groups, width), 1) // GROUP
        rate = jnp.sum(jnp.where(at_group, picked, 0.0), axis=0, keepdims=True)
        decay = jnp.exp(-rate * float(rows))
        held = jnp.zeros((1, width), F32)
        out_ref[r] = held
        for n in range(1, chunks):
            out_ref[n * each + r] = held
            held = decay * held + state_ref[(n - 1) * each + r]


def dot_rows(a, b):
    return lax.dot_general(a, b, (((1,), (1,)), ((), ())), preferred_element_type=F32)


def local_kernel(
    border_ref,
    key_ref,
    value_ref,
    filter_ref,
    rate_ref,
    residue_ref,
    skip_ref,
    base_ref,
    factor_ref,
    product_window,
    mixed_window,
    turned,
):
    samples, rows, _ = key_ref.shape
    modes = rate_ref.shape[0]
    taps = filter_ref.shape[1]
    span = rows + taps
    blocks = rows // taps
    before = span - 2 * taps
    tile = pl.program_id(0)
    rate = tile_column(rate_ref[...], tile)
    residue = tile_column(residue_ref[...], tile)
    filters = filter_ref[...]

    reverse = (iota((taps, 2 * taps), 0) + iota((taps, 2 * taps), 1) == taps).astype(BF16)
    short_base = dot(filters, reverse)
    wide = span + taps
    place = iota((1, wide), 1)
    lag = jnp.where(place <= rows, rows - place, rows + wide - place)
    zero = jnp.logical_and(place > rows, place <= span)
    modal = residue * jnp.exp(-rate * lag.astype(F32))
    modal = jnp.where(zero, 0.0, modal)
    long_base = jnp.sum(modal.reshape(TILE_GROUPS, modes, wide), axis=1)

    for s in range(samples):
        product_window[s, :, :taps] = jnp.zeros((LANES, taps), BF16)
        mixed_window[s, :, :before] = jnp.zeros((LANES, before), BF16)
        border = border_ref[s * taps : (s + 1) * taps, :].astype(F32)
        product_window[s, :, taps : 2 * taps] = border.T.astype(BF16)
        product = product_of(key_ref[s], value_ref[s]).astype(F32)
        product_window[s, :, 2 * taps :] = product.T.astype(BF16)

    skip = jnp.broadcast_to(skip_ref[...], (8, LANES)).T[:, :1]
    for g in range(TILE_GROUPS):
        channels = slice(g * GROUP, (g + 1) * GROUP)
        spread = jnp.broadcast_to(short_base[g : g + 1], (taps, 2 * taps))
        short_table = pltpu.roll(spread, 0, 1, stride=1, stride_axis=0).astype(BF16)
        pieces = [
            product_window[s, channels, b * taps : (b + 2) * taps]
            for s in range(samples)
            for b in range(blocks + 1)
        ]
        mixed = dot_rows(jnp.concatenate(pieces, axis=0), short_table).astype(BF16)
        for s in range(samples):
            for b in range(blocks + 1):
                first = (s * (blocks + 1) + b) * GROUP
                mixed_window[s, channels, before + b * taps : before + (b + 1) * taps] = mixed[
                    first : first + GROUP
                ]
        spread = jnp.broadcast_to(long_base[g : g + 1], (taps, wide))
        long_table = pltpu.roll(spread, 0, 1, stride=1, stride_axis=0)[:, :span].astype(BF16)
        pieces = [
            mixed_window[s, channels, b * taps : b * taps + span]
            for s in range(samples)
            for b in range(blocks)
        ]
        filtered = dot_rows(jnp.concatenate(pieces, axis=0), long_table)
        for s in range(samples):
            for b in range(blocks):
                first = (s * blocks + b) * GROUP
                at = (s * (blocks + 1) + b + 1) * GROUP
                turned[s, channels, b * taps : (b + 1) * taps] = filtered[
                    first : first + GROUP
                ] + skip[channels] * mixed[at : at + GROUP].astype(F32)
    for s in range(samples):
        base_ref[s] = turned[s].T.astype(BF16)

    tap_weights = jnp.exp(-rate * (taps - iota((1, taps), 1, F32)))
    spread = jnp.broadcast_to(
        filters.astype(F32)[:, None, :], (TILE_GROUPS, modes, taps)
    ).reshape(TILE_GROUPS * modes, taps)
    gain = residue * jnp.sum(spread * tap_weights, axis=1, keepdims=True)
    square = (TILE_GROUPS * modes, LANES)
    factor_ref[:modes, :] = own_group(
        jnp.broadcast_to(jnp.exp(-rate * float(rows - taps)), square), modes
    )
    factor_ref[modes:, :] = own_group(jnp.broadcast_to(gain, square), modes)


def embed_kernel(token_ref, table_ref, out_ref):
    samples, rows = token_ref.shape
    vocab = table_ref.shape[0]
    for s in range(samples):
        ids = jnp.broadcast_to(token_ref[s : s + 1, :].astype(F32), (8, rows)).T[:, :1]
        one_hot = (ids == iota((rows, vocab), 1, F32)).astype(BF16)
        out_ref[s] = dot(one_hot, table_ref[...]).astype(BF16)


def gate_kernel(
    carried_ref,
    before_ref,
    factor_ref,
    rate_ref,
    base_source,
    query_source,
    gated_ref,
    sum_ref,
    base_ref,
    query_ref,
    squares,
    arrived,
):
    samples, rows, width = base_ref.shape
    modes = factor_ref.shape[0] // 2
    copies = sum_ref.shape[0]
    early_at = before_ref.shape[0] - 2 * samples * modes
    own = iota((LANES, LANES), 0) // modes == iota((LANES, LANES), 1) // GROUP
    tiles = [slice(first, first + LANES) for first in range(0, width, LANES)]
    loads = []
    for tile, lanes in enumerate(tiles):
        pair = (
            pltpu.make_async_copy(
                base_source.at[:, :, lanes], base_ref.at[:, :, lanes], arrived.at[0, tile]
            ),
            pltpu.make_async_copy(
                query_source.at[:, :, lanes], query_ref.at[:, :, lanes], arrived.at[1, tile]
            ),
        )
        for load in pair:
            load.start()
        loads.append(pair)
    for tile, lanes in enumerate(tiles):
        rate = rate_ref[:, lanes]
        head = jnp.exp(-rate * (1.0 + iota((LANES, 1), 0, F32)))
        step = jnp.exp(-rate * float(LANES))
        after = [head]
        for _ in range(rows // LANES - 1):
            after.append(after[-1] * step)
        upper, lower = halves(jnp.concatenate(after, axis=0))
        after = jnp.concatenate([upper, lower, upper], axis=1)
        for load in loads[tile]:
            load.wait()
        for s in range(samples):
            part = slice(s * modes, (s + 1) * modes)
            carried = carried_ref[part, :, lanes].reshape(modes, LANES)
            first = early_at + s * modes
            early = before_ref[first : first + modes, lanes].astype(F32)
            first = first + samples * modes
            early = early + before_ref[first : first + modes, lanes].astype(F32)
            state = factor_ref[:modes, lanes] * carried + early
            state = state * factor_ref[modes:, lanes]
            spread = jnp.concatenate([state] * TILE_GROUPS, axis=0)
            upper, lower = halves(jnp.where(own, spread, 0.0))
            carry = dot(after, jnp.concatenate([upper, upper, lower], axis=0))
            base = base_ref[s, :, lanes].astype(F32)
            gated = query_ref[s, :, lanes].astype(F32) * (base + carry)
            gated_ref[s, :, lanes] = gated
            if tile == 0:
                squares[s] = gated * gated
            else:
                squares[s] = squares[s] + gated * gated
    for s in range(samples):
        total = jnp.sum(squares[s].T, axis=0, keepdims=True)
        sum_ref[:, :, s * rows : (s + 1) * rows] = jnp.broadcast_to(
            total.reshape(1, 1, rows), (copies, 1, rows)
        )


def norm_kernel(
    length_ref, index_ref, sum_ref, gated_ref, embed_ref, gain_ref, out_target, out_ref, left, *, full
):
    samples, rows, _ = gated_ref.shape
    here = 128
    total = jnp.sum(sum_ref[...], axis=0)
    scale = jnp.broadcast_to(lax.rsqrt(total / full + 1e-06), (8, samples * rows)).T[:, :1]
    stores = []
    for s in range(samples):
        for part in range(rows // here):
            at = slice(part * here, (part + 1) * here)
            start = index_ref[0] * rows + part * here
            valid = start + iota((here, 1), 0) < length_ref[s]
            first = s * rows + part * here
            value = gated_ref[s, at, :] * scale[first : first + here] * gain_ref[...]
            value = value + embed_ref[s, at, :].astype(F32)
            out_ref[s, at, :] = jnp.where(valid, value, 0.0).astype(BF16)
            store = pltpu.make_async_copy(
                out_ref.at[s, at, :], out_target.at[s, at, :], left.at[s, part]
            )
            store.start()
            stores.append(store)
    for store in stores:
        store.wait()


def params(mebibytes):
    return pltpu.CompilerParams(vmem_limit_bytes=int(mebibytes * (1 << 20)))


def per_device(
    token_ids,
    lengths,
    embedding,
    query_act,
    key_act,
    value_act,
    short_filter,
    decay_rates,
    residues,
    skip_gain,
    norm_gain,
):
    samples, rows, width = query_act.shape
    taps = short_filter.shape[1]
    groups, modes = decay_rates.shape
    vocab = embedding.shape[0]
    chunks = lax.axis_size("ctx")
    columns = lax.axis_size("tp")
    index = lax.axis_index("ctx").reshape(1)
    tiles = width // LANES
    smem = pl.BlockSpec(memory_space=pltpu.SMEM)

    def cube():
        return pl.BlockSpec((samples, rows, LANES), lambda i: (0, 0, i))

    def flat(height):
        return pl.BlockSpec((height, LANES), lambda i: (0, i))

    def grouped(cols):
        return pl.BlockSpec((TILE_GROUPS, cols), lambda i: (i, 0))

    state_rows = samples * modes
    border_rows = samples * taps + 2 * state_rows
    shape = jax.ShapeDtypeStruct
    whole = pl.BlockSpec((modes, groups), lambda i: (0, 0))
    rates = decay_rates.T

    vmem = pl.BlockSpec(memory_space=pltpu.VMEM)
    anywhere = pl.BlockSpec(memory_space=pl.ANY)

    def states_step(*refs):
        states_kernel(*refs, taps=taps)

    states, border = pl.pallas_call(
        states_step,
        in_specs=[vmem, anywhere, anywhere],
        out_shape=[
            shape((state_rows, 1, width), F32),
            shape((border_rows, width), BF16),
        ],
        scratch_shapes=[
            pltpu.VMEM((samples, rows, width), BF16),
            pltpu.VMEM((samples, rows, width), BF16),
            pltpu.SemaphoreType.DMA((2, tiles)),
        ],
        compiler_params=params(60),
        name="states",
    )(rates, key_act, value_act)
    before = lax.ppermute(border, "ctx", [(i, i + 1) for i in range(chunks - 1)])
    gathered = lax.all_to_all(states, "ctx", split_axis=0, concat_axis=0, tiled=True)

    embedded = pl.pallas_call(
        embed_kernel,
        out_shape=shape((samples, rows, width), BF16),
        cost_estimate=pl.CostEstimate(
            flops=2 * samples * rows * width * vocab, bytes_accessed=4 << 20, transcendentals=0
        ),
        compiler_params=params(16),
        name="embed",
    )(token_ids, embedding)

    base, factors = pl.pallas_call(
        local_kernel,
        grid=(tiles,),
        in_specs=[flat(border_rows), cube(), cube(), grouped(taps), whole, whole, flat(1)],
        out_specs=[cube(), flat(2 * modes)],
        out_shape=[
            shape((samples, rows, width), BF16),
            shape((2 * modes, width), F32),
        ],
        scratch_shapes=[
            pltpu.VMEM((samples, LANES, rows + 2 * taps), BF16),
            pltpu.VMEM((samples, LANES, 2 * rows), BF16),
            pltpu.VMEM((samples, LANES, rows), F32),
        ],
        cost_estimate=pl.CostEstimate(
            flops=12_000_000_000, bytes_accessed=8 << 20, transcendentals=1 << 20
        ),
        compiler_params=params(60),
        name="local",
    )(
        before,
        key_act,
        value_act,
        short_filter,
        rates,
        residues.T,
        skip_gain.reshape(1, width),
    )

    def scan(first_ref, rate_ref, state_ref, out_ref):
        scan_kernel(first_ref, rate_ref, state_ref, out_ref, chunks=chunks, rows=rows)

    entering = pl.pallas_call(
        scan,
        in_specs=[smem, vmem, vmem],
        out_shape=shape((state_rows, 1, width), F32),
        compiler_params=params(8),
        name="scan",
    )(index, decay_rates, gathered)
    carried = lax.all_to_all(entering, "ctx", split_axis=0, concat_axis=0, tiled=True)

    gated, sums = pl.pallas_call(
        gate_kernel,
        in_specs=[vmem, vmem, vmem, vmem, anywhere, anywhere],
        out_shape=[
            shape((samples, rows, width), F32),
            shape((columns, 1, samples * rows), F32),
        ],
        scratch_shapes=[
            pltpu.VMEM((samples, rows, width), BF16),
            pltpu.VMEM((samples, rows, width), BF16),
            pltpu.VMEM((samples, rows, LANES), F32),
            pltpu.SemaphoreType.DMA((2, tiles)),
        ],
        compiler_params=params(16),
        name="gate",
    )(carried, before, factors, decay_rates.reshape(1, groups * modes), base, query_act)
    shares = lax.all_to_all(sums, "tp", split_axis=0, concat_axis=0, tiled=True)

    def norm(*refs):
        norm_kernel(*refs, full=float(columns * width))

    return pl.pallas_call(
        norm,
        in_specs=[smem, smem, vmem, vmem, vmem, vmem],
        out_specs=anywhere,
        out_shape=shape((samples, rows, width), BF16),
        scratch_shapes=[
            pltpu.VMEM((samples, rows, width), BF16),
            pltpu.SemaphoreType.DMA((samples, rows // 128)),
        ],
        compiler_params=params(16),
        name="norm",
    )(lengths, index, shares, gated, embedded, norm_gain.reshape(1, width))


def solution(mesh):
    placed = (
        P(None, "ctx"),
        P(),
        P(None, "tp"),
        P(None, "ctx", "tp"),
        P(None, "ctx", "tp"),
        P(None, "ctx", "tp"),
        P("tp", None),
        P("tp", None),
        P("tp", None),
        P("tp"),
        P("tp"),
    )
    return jax.shard_map(
        per_device, mesh=mesh, in_specs=placed, out_specs=P(None, "ctx", "tp"), check_vma=False
    )
```

```python
import jax
import jax.numpy as jnp
from jax import lax
from jax.experimental import pallas as pl
from jax.experimental.pallas import tpu as pltpu
from jax.sharding import PartitionSpec as P

GROUP = 16
LANES = 128
TILE_GROUPS = LANES // GROUP
F32 = jnp.float32
BF16 = jnp.bfloat16


def iota(shape, dim, dtype=jnp.int32):
    return lax.broadcasted_iota(jnp.int32, shape, dim).astype(dtype)


def own_group(stacked, rows):
    lane_group = iota((rows, LANES), 1) // GROUP
    picked = stacked[:rows]
    for g in range(1, TILE_GROUPS):
        picked = jnp.where(lane_group == g, stacked[g * rows : (g + 1) * rows], picked)
    return picked


def halves(values):
    upper = values.astype(BF16)
    return upper, (values - upper.astype(F32)).astype(BF16)


def dot(a, b):
    return jnp.dot(a, b, preferred_element_type=F32)


def tile_column(table, tile):
    modes, groups = table.shape
    parts = []
    for g in range(TILE_GROUPS):
        here = iota((modes, groups), 1) == tile * TILE_GROUPS + g
        parts.append(jnp.sum(jnp.where(here, table, 0.0), axis=1, keepdims=True))
    return jnp.concatenate(parts, axis=0)


def product_of(key, value):
    return (key.astype(F32) * value.astype(F32)).astype(BF16)


def states_kernel(
    rate_source,
    key_source,
    value_source,
    state_target,
    border_target,
    rate_ref,
    key_ref,
    value_ref,
    state_ref,
    border_ref,
    ready,
    arrived,
    left,
    *,
    taps,
):
    samples, rows, width = key_ref.shape
    modes = rate_ref.shape[0]
    tiles = [slice(first, first + LANES) for first in range(0, width, LANES)]
    rate_load = pltpu.make_async_copy(rate_source, rate_ref, ready.at[0])
    rate_load.start()
    loads, stores = [], []
    for tile, lanes in enumerate(tiles):
        pair = (
            pltpu.make_async_copy(
                key_source.at[:, :, lanes], key_ref.at[:, :, lanes], arrived.at[0, tile]
            ),
            pltpu.make_async_copy(
                value_source.at[:, :, lanes], value_ref.at[:, :, lanes], arrived.at[1, tile]
            ),
        )
        for load in pair:
            load.start()
        loads.append(pair)
    rate_load.wait()
    tables = []
    for tile in range(len(tiles)):
        groups = range(tile * TILE_GROUPS, (tile + 1) * TILE_GROUPS)
        rate = jnp.concatenate([rate_ref[:, g : g + 1] for g in groups], axis=0)
        weights = [jnp.exp(-rate * (taps - 1.0 - iota((1, taps), 1, F32)))]
        step = jnp.exp(-rate * float(taps))
        for _ in range(rows // taps - 1):
            weights.insert(0, weights[0] * step)
        tables.append(jnp.concatenate(halves(jnp.concatenate(weights, axis=1)), axis=0))
    for tile, lanes in enumerate(tiles):
        weights = tables[tile]
        half = weights.shape[0] // 2
        for load in loads[tile]:
            load.wait()
        for s in range(samples):
            product = product_of(key_ref[s, :, lanes], value_ref[s, :, lanes])
            full = dot(weights, product)
            state = own_group(full[:half] + full[half:], modes)
            state_ref[s * modes : (s + 1) * modes, :, lanes] = state.reshape(modes, 1, LANES)
            border_ref[s * taps : (s + 1) * taps, lanes] = product[rows - taps :]
            early = dot(weights[:, taps:], product[: rows - taps])
            upper, lower = halves(own_group(early[:half] + early[half:], modes))
            first = samples * taps + s * modes
            border_ref[first : first + modes, lanes] = upper
            border_ref[first + samples * modes : first + (samples + 1) * modes, lanes] = lower
        pair = (
            pltpu.make_async_copy(
                state_ref.at[:, :, lanes], state_target.at[:, :, lanes], left.at[0, tile]
            ),
            pltpu.make_async_copy(
                border_ref.at[:, lanes], border_target.at[:, lanes], left.at[1, tile]
            ),
        )
        for store in pair:
            store.start()
            stores.append(store)
    for store in stores:
        store.wait()


def scan_kernel(first_ref, rate_ref, state_ref, out_ref, *, chunks, rows):
    total, _, width = state_ref.shape
    each = total // chunks
    groups, modes = rate_ref.shape
    rates = rate_ref[...]
    for r in range(each):
        mode = lax.rem(first_ref[0] * each + r, modes)
        picked = jnp.sum(
            jnp.where(iota(rates.shape, 1) == mode, rates, 0.0), axis=1, keepdims=True
        )
        at_group = iota((groups, width), 0) == iota((groups, width), 1) // GROUP
        rate = jnp.sum(jnp.where(at_group, picked, 0.0), axis=0, keepdims=True)
        decay = jnp.exp(-rate * float(rows))
        held = jnp.zeros((1, width), F32)
        out_ref[r] = held
        for n in range(1, chunks):
            out_ref[n * each + r] = held
            held = decay * held + state_ref[(n - 1) * each + r]


def dot_rows(a, b):
    return lax.dot_general(a, b, (((1,), (1,)), ((), ())), preferred_element_type=F32)


def local_kernel(
    index_ref,
    border_ref,
    key_ref,
    value_ref,
    filter_ref,
    rate_ref,
    residue_ref,
    skip_ref,
    base_ref,
    turn_ref,
    product_window,
    mixed_window,
    turned,
):
    samples, rows, _ = key_ref.shape
    modes = rate_ref.shape[0]
    taps = filter_ref.shape[1]
    span = rows + taps
    blocks = rows // taps
    before = span - 2 * taps
    tile = pl.program_id(0)
    rate = tile_column(rate_ref[...], tile)
    residue = tile_column(residue_ref[...], tile)
    filters = filter_ref[...]

    reverse = (iota((taps, 2 * taps), 0) + iota((taps, 2 * taps), 1) == taps).astype(BF16)
    short_base = dot(filters, reverse)
    wide = span + taps
    place = iota((1, wide), 1)
    lag = jnp.where(place <= rows, rows - place, rows + wide - place)
    zero = jnp.logical_and(place > rows, place <= span)
    modal = residue * jnp.exp(-rate * lag.astype(F32))
    modal = jnp.where(zero, 0.0, modal)
    long_base = jnp.sum(modal.reshape(TILE_GROUPS, modes, wide), axis=1)

    for s in range(samples):
        product_window[s, :, :taps] = jnp.zeros((LANES, taps), BF16)
        mixed_window[s, :, :before] = jnp.zeros((LANES, before), BF16)
        border = border_ref[s * taps : (s + 1) * taps, :].astype(F32)
        product_window[s, :, taps : 2 * taps] = border.T.astype(BF16)
        product = product_of(key_ref[s], value_ref[s]).astype(F32)
        product_window[s, :, 2 * taps :] = product.T.astype(BF16)

    skip = jnp.broadcast_to(skip_ref[...], (8, LANES)).T[:, :1]
    for g in range(TILE_GROUPS):
        channels = slice(g * GROUP, (g + 1) * GROUP)
        spread = jnp.broadcast_to(short_base[g : g + 1], (taps, 2 * taps))
        short_table = pltpu.roll(spread, 0, 1, stride=1, stride_axis=0).astype(BF16)
        pieces = [
            product_window[s, channels, b * taps : (b + 2) * taps]
            for s in range(samples)
            for b in range(blocks + 1)
        ]
        mixed = dot_rows(jnp.concatenate(pieces, axis=0), short_table).astype(BF16)
        for s in range(samples):
            for b in range(blocks + 1):
                first = (s * (blocks + 1) + b) * GROUP
                mixed_window[s, channels, before + b * taps : before + (b + 1) * taps] = mixed[
                    first : first + GROUP
                ]
        spread = jnp.broadcast_to(long_base[g : g + 1], (taps, wide))
        long_table = pltpu.roll(spread, 0, 1, stride=1, stride_axis=0)[:, :span].astype(BF16)
        pieces = [
            mixed_window[s, channels, b * taps : b * taps + span]
            for s in range(samples)
            for b in range(blocks)
        ]
        filtered = dot_rows(jnp.concatenate(pieces, axis=0), long_table)
        for s in range(samples):
            for b in range(blocks):
                first = (s * blocks + b) * GROUP
                at = (s * (blocks + 1) + b + 1) * GROUP
                turned[s, channels, b * taps : (b + 1) * taps] = filtered[
                    first : first + GROUP
                ] + skip[channels] * mixed[at : at + GROUP].astype(F32)
    for s in range(samples):
        base_ref[s * rows : (s + 1) * rows, :] = turned[s].T.astype(BF16)

    tap_weights = jnp.exp(-rate * (taps - iota((1, taps), 1, F32)))
    spread = jnp.broadcast_to(
        filters.astype(F32)[:, None, :], (TILE_GROUPS, modes, taps)
    ).reshape(TILE_GROUPS * modes, taps)
    gain = residue * jnp.sum(spread * tap_weights, axis=1, keepdims=True)
    square = (TILE_GROUPS * modes, LANES)
    decay = own_group(jnp.broadcast_to(jnp.exp(-rate * float(rows - taps)), square), modes)
    gain = own_group(jnp.broadcast_to(gain, square), modes)
    first, state_rows = samples * taps, samples * modes
    early = border_ref[first : first + state_rows, :].astype(F32)
    early = early + border_ref[first + state_rows :, :].astype(F32)
    factors = jnp.concatenate([decay, gain, early], axis=0)
    base_ref[samples * rows :, :] = jnp.concatenate(halves(factors), axis=0)
    turn_ref[0] = index_ref[0]


def embed_kernel(token_ref, table_ref, out_ref):
    samples, rows = token_ref.shape
    vocab = table_ref.shape[0]
    for s in range(samples):
        ids = jnp.broadcast_to(token_ref[s : s + 1, :].astype(F32), (8, rows)).T[:, :1]
        one_hot = (ids == iota((rows, vocab), 1, F32)).astype(BF16)
        out_ref[s] = dot(one_hot, table_ref[...]).astype(BF16)


def gate_kernel(
    carried_ref, rate_ref, base_ref, query_ref, gated_ref, sum_ref, squares
):
    samples, rows, width = query_ref.shape
    height = (base_ref.shape[0] - samples * rows) // 2
    modes = carried_ref.shape[0] // samples
    copies = sum_ref.shape[0]
    own = iota((LANES, LANES), 0) // modes == iota((LANES, LANES), 1) // GROUP
    for tile in range(width // LANES):
        lanes = slice(tile * LANES, (tile + 1) * LANES)
        rate = rate_ref[:, lanes]
        head = jnp.exp(-rate * (1.0 + iota((LANES, 1), 0, F32)))
        step = jnp.exp(-rate * float(LANES))
        after = [head]
        for _ in range(rows // LANES - 1):
            after.append(after[-1] * step)
        upper, lower = halves(jnp.concatenate(after, axis=0))
        after = jnp.concatenate([upper, lower, upper], axis=1)
        factors = base_ref[samples * rows :, lanes].astype(F32)
        factors = factors[:height] + factors[height:]
        for s in range(samples):
            carried = carried_ref[s * modes : (s + 1) * modes, :, lanes].reshape(modes, LANES)
            early = factors[(s + 2) * modes : (s + 3) * modes]
            state = (factors[:modes] * carried + early) * factors[modes : 2 * modes]
            spread = jnp.concatenate([state] * TILE_GROUPS, axis=0)
            upper, lower = halves(jnp.where(own, spread, 0.0))
            carry = dot(after, jnp.concatenate([upper, upper, lower], axis=0))
            base = base_ref[s * rows : (s + 1) * rows, lanes].astype(F32)
            gated = query_ref[s, :, lanes].astype(F32) * (base + carry)
            gated_ref[s, :, lanes] = gated
            if tile == 0:
                squares[s] = gated * gated
            else:
                squares[s] = squares[s] + gated * gated
    for s in range(samples):
        total = jnp.sum(squares[s].T, axis=0, keepdims=True)
        sum_ref[:, :, s * rows : (s + 1) * rows] = jnp.broadcast_to(
            total.reshape(1, 1, rows), (copies, 1, rows)
        )


def norm_kernel(
    length_ref, index_ref, sum_ref, gated_ref, embed_ref, gain_ref, out_target, out_ref, left, *, full
):
    samples, rows, _ = gated_ref.shape
    here = 128
    total = jnp.sum(sum_ref[...], axis=0)
    scale = jnp.broadcast_to(lax.rsqrt(total / full + 1e-06), (8, samples * rows)).T[:, :1]
    stores = []
    for s in range(samples):
        for part in range(rows // here):
            at = slice(part * here, (part + 1) * here)
            start = index_ref[0] * rows + part * here
            valid = start + iota((here, 1), 0) < length_ref[s]
            first = s * rows + part * here
            value = gated_ref[s, at, :] * scale[first : first + here] * gain_ref[...]
            value = value + embed_ref[s, at, :].astype(F32)
            out_ref[s, at, :] = jnp.where(valid, value, 0.0).astype(BF16)
            store = pltpu.make_async_copy(
                out_ref.at[s, at, :], out_target.at[s, at, :], left.at[s, part]
            )
            store.start()
            stores.append(store)
    for store in stores:
        store.wait()


def params(mebibytes):
    return pltpu.CompilerParams(vmem_limit_bytes=int(mebibytes * (1 << 20)))


def per_device(
    token_ids,
    lengths,
    embedding,
    query_act,
    key_act,
    value_act,
    short_filter,
    decay_rates,
    residues,
    skip_gain,
    norm_gain,
):
    samples, rows, width = query_act.shape
    taps = short_filter.shape[1]
    groups, modes = decay_rates.shape
    vocab = embedding.shape[0]
    chunks = lax.axis_size("ctx")
    columns = lax.axis_size("tp")
    index = lax.axis_index("ctx").reshape(1)
    tiles = width // LANES
    smem = pl.BlockSpec(memory_space=pltpu.SMEM)

    def cube():
        return pl.BlockSpec((samples, rows, LANES), lambda i: (0, 0, i))

    def flat(height):
        return pl.BlockSpec((height, LANES), lambda i: (0, i))

    def grouped(cols):
        return pl.BlockSpec((TILE_GROUPS, cols), lambda i: (i, 0))

    state_rows = samples * modes
    border_rows = samples * taps + 2 * state_rows
    base_rows = samples * rows + 2 * (2 * modes + state_rows)
    shape = jax.ShapeDtypeStruct
    whole = pl.BlockSpec((modes, groups), lambda i: (0, 0))
    rates = decay_rates.T

    vmem = pl.BlockSpec(memory_space=pltpu.VMEM)
    anywhere = pl.BlockSpec(memory_space=pl.ANY)

    def states_step(*refs):
        states_kernel(*refs, taps=taps)

    states, border = pl.pallas_call(
        states_step,
        in_specs=[anywhere, anywhere, anywhere],
        out_specs=[anywhere, anywhere],
        out_shape=[
            shape((state_rows, 1, width), F32),
            shape((border_rows, width), BF16),
        ],
        scratch_shapes=[
            pltpu.VMEM((modes, groups), F32),
            pltpu.VMEM((samples, rows, width), BF16),
            pltpu.VMEM((samples, rows, width), BF16),
            pltpu.VMEM((state_rows, 1, width), F32),
            pltpu.VMEM((border_rows, width), BF16),
            pltpu.SemaphoreType.DMA((1,)),
            pltpu.SemaphoreType.DMA((2, tiles)),
            pltpu.SemaphoreType.DMA((2, tiles)),
        ],
        compiler_params=params(60),
        name="states",
    )(rates, key_act, value_act)
    before = lax.ppermute(border, "ctx", [(i, i + 1) for i in range(chunks - 1)])
    gathered = lax.all_to_all(states, "ctx", split_axis=0, concat_axis=0, tiled=True)

    embedded = pl.pallas_call(
        embed_kernel,
        out_shape=shape((samples, rows, width), BF16),
        cost_estimate=pl.CostEstimate(
            flops=2 * samples * rows * width * vocab, bytes_accessed=4 << 20, transcendentals=0
        ),
        compiler_params=params(16),
        name="embed",
    )(token_ids, embedding)

    base, turn = pl.pallas_call(
        local_kernel,
        grid=(tiles,),
        in_specs=[smem, flat(border_rows), cube(), cube(), grouped(taps), whole, whole, flat(1)],
        out_specs=[flat(base_rows), smem],
        out_shape=[
            shape((base_rows, width), BF16),
            shape((1,), jnp.int32),
        ],
        scratch_shapes=[
            pltpu.VMEM((samples, LANES, rows + 2 * taps), BF16),
            pltpu.VMEM((samples, LANES, 2 * rows), BF16),
            pltpu.VMEM((samples, LANES, rows), F32),
        ],
        cost_estimate=pl.CostEstimate(
            flops=12_000_000_000, bytes_accessed=8 << 20, transcendentals=1 << 20
        ),
        compiler_params=params(60),
        name="local",
    )(
        index,
        before,
        key_act,
        value_act,
        short_filter,
        rates,
        residues.T,
        skip_gain.reshape(1, width),
    )

    def scan(first_ref, rate_ref, state_ref, out_ref):
        scan_kernel(first_ref, rate_ref, state_ref, out_ref, chunks=chunks, rows=rows)

    entering = pl.pallas_call(
        scan,
        in_specs=[smem, vmem, vmem],
        out_shape=shape((state_rows, 1, width), F32),
        compiler_params=params(8),
        name="scan",
    )(turn, decay_rates, gathered)
    carried = lax.all_to_all(entering, "ctx", split_axis=0, concat_axis=0, tiled=True)

    gated, sums = pl.pallas_call(
        gate_kernel,
        out_shape=[
            shape((samples, rows, width), F32),
            shape((columns, 1, samples * rows), F32),
        ],
        scratch_shapes=[
            pltpu.VMEM((samples, rows, LANES), F32),
        ],
        compiler_params=params(16),
        name="gate",
    )(carried, decay_rates.reshape(1, groups * modes), base, query_act)
    shares = lax.all_to_all(sums, "tp", split_axis=0, concat_axis=0, tiled=True)

    def norm(*refs):
        norm_kernel(*refs, full=float(columns * width))

    return pl.pallas_call(
        norm,
        in_specs=[smem, smem, vmem, vmem, vmem, vmem],
        out_specs=anywhere,
        out_shape=shape((samples, rows, width), BF16),
        scratch_shapes=[
            pltpu.VMEM((samples, rows, width), BF16),
            pltpu.SemaphoreType.DMA((samples, rows // 128)),
        ],
        compiler_params=params(16),
        name="norm",
    )(lengths, index, shares, gated, embedded, norm_gain.reshape(1, width))


def solution(mesh):
    placed = (
        P(None, "ctx"),
        P(),
        P(None, "tp"),
        P(None, "ctx", "tp"),
        P(None, "ctx", "tp"),
        P(None, "ctx", "tp"),
        P("tp", None),
        P("tp", None),
        P("tp", None),
        P("tp"),
        P("tp"),
    )
    return jax.shard_map(
        per_device, mesh=mesh, in_specs=placed, out_specs=P(None, "ctx", "tp"), check_vma=False
    )
```

```python
import jax
import jax.numpy as jnp
from jax import lax
from jax.experimental import pallas as pl
from jax.experimental.pallas import tpu as pltpu
from jax.sharding import PartitionSpec as P

GROUP = 16
LANES = 128
TILE_GROUPS = LANES // GROUP
F32 = jnp.float32
BF16 = jnp.bfloat16


def iota(shape, dim, dtype=jnp.int32):
    return lax.broadcasted_iota(jnp.int32, shape, dim).astype(dtype)


def own_group(stacked, rows):
    lane_group = iota((rows, LANES), 1) // GROUP
    picked = stacked[:rows]
    for g in range(1, TILE_GROUPS):
        picked = jnp.where(lane_group == g, stacked[g * rows : (g + 1) * rows], picked)
    return picked


def halves(values):
    upper = values.astype(BF16)
    return upper, (values - upper.astype(F32)).astype(BF16)


def dot(a, b):
    return jnp.dot(a, b, preferred_element_type=F32)


def tile_column(table, tile):
    modes, groups = table.shape
    parts = []
    for g in range(TILE_GROUPS):
        here = iota((modes, groups), 1) == tile * TILE_GROUPS + g
        parts.append(jnp.sum(jnp.where(here, table, 0.0), axis=1, keepdims=True))
    return jnp.concatenate(parts, axis=0)


def product_of(key, value):
    return (key.astype(F32) * value.astype(F32)).astype(BF16)


def states_kernel(
    rate_source,
    key_source,
    value_source,
    state_target,
    border_target,
    rate_ref,
    key_ref,
    value_ref,
    state_ref,
    border_ref,
    ready,
    arrived,
    left,
    *,
    taps,
):
    samples, rows, width = key_ref.shape
    modes = rate_ref.shape[0]
    tiles = [slice(first, first + LANES) for first in range(0, width, LANES)]
    rate_load = pltpu.make_async_copy(rate_source, rate_ref, ready.at[0])
    rate_load.start()
    loads, stores = [], []
    for tile, lanes in enumerate(tiles):
        pair = (
            pltpu.make_async_copy(
                key_source.at[:, :, lanes], key_ref.at[:, :, lanes], arrived.at[0, tile]
            ),
            pltpu.make_async_copy(
                value_source.at[:, :, lanes], value_ref.at[:, :, lanes], arrived.at[1, tile]
            ),
        )
        for load in pair:
            load.start()
        loads.append(pair)
    rate_load.wait()
    tables = []
    for tile in range(len(tiles)):
        groups = range(tile * TILE_GROUPS, (tile + 1) * TILE_GROUPS)
        rate = jnp.concatenate([rate_ref[:, g : g + 1] for g in groups], axis=0)
        weights = [jnp.exp(-rate * (taps - 1.0 - iota((1, taps), 1, F32)))]
        step = jnp.exp(-rate * float(taps))
        for _ in range(rows // taps - 1):
            weights.insert(0, weights[0] * step)
        tables.append(jnp.concatenate(halves(jnp.concatenate(weights, axis=1)), axis=0))
    for tile, lanes in enumerate(tiles):
        weights = tables[tile]
        half = weights.shape[0] // 2
        for load in loads[tile]:
            load.wait()
        for s in range(samples):
            product = product_of(key_ref[s, :, lanes], value_ref[s, :, lanes])
            full = dot(weights, product)
            state = own_group(full[:half] + full[half:], modes)
            state = state.astype(BF16)
            for copy in range(state_ref.shape[0] // (samples * modes)):
                at = (copy * samples + s) * modes
                state_ref[at : at + modes, lanes] = state
            border_ref[s * taps : (s + 1) * taps, lanes] = product[rows - taps :]
            early = dot(weights[:, taps:], product[: rows - taps])
            upper, lower = halves(own_group(early[:half] + early[half:], modes))
            first = samples * taps + s * modes
            border_ref[first : first + modes, lanes] = upper
            border_ref[first + samples * modes : first + (samples + 1) * modes, lanes] = lower
        pair = (
            pltpu.make_async_copy(
                state_ref.at[:, lanes], state_target.at[:, lanes], left.at[0, tile]
            ),
            pltpu.make_async_copy(
                border_ref.at[:, lanes], border_target.at[:, lanes], left.at[1, tile]
            ),
        )
        for store in pair:
            store.start()
            stores.append(store)
    for store in stores:
        store.wait()


def group_kernel(index_ref, rate_ref, state_ref, far_ref, own_ref, *, near, rows):
    height = own_ref.shape[0]
    far = far_ref.shape[0] // height
    modes = rate_ref.shape[0]
    group, place = index_ref[0] // near, lax.rem(index_ref[0], near)
    rate = jnp.concatenate([rate_ref[...]] * (height // modes), axis=0) * float(rows)
    decay = jnp.exp(-rate)
    held = jnp.zeros(own_ref.shape, F32)
    own, short = held, held
    for p in range(near):
        own = jnp.where(place == p + 1, held, own)
        short = held
        held = decay * held + state_ref[p * height : (p + 1) * height, :].astype(F32)
    own_ref[...] = own
    for other in range(far):
        ahead = (other - group) * near + place - near - 1
        weight = jnp.exp(-rate * jnp.maximum(ahead, 0).astype(F32))
        value = jnp.where(ahead < 0, short, weight * held)
        value = jnp.where(other > group, value, 0.0)
        far_ref[other * height : (other + 1) * height, :] = value.astype(BF16)


def dot_rows(a, b):
    return lax.dot_general(a, b, (((1,), (1,)), ((), ())), preferred_element_type=F32)


def local_kernel(
    border_ref,
    key_ref,
    value_ref,
    filter_ref,
    rate_ref,
    residue_ref,
    skip_ref,
    base_ref,
    product_window,
    mixed_window,
    turned,
):
    samples, rows, _ = key_ref.shape
    modes = rate_ref.shape[0]
    taps = filter_ref.shape[1]
    span = rows + taps
    blocks = rows // taps
    before = span - 2 * taps
    tile = pl.program_id(0)
    rate = tile_column(rate_ref[...], tile)
    residue = tile_column(residue_ref[...], tile)
    filters = filter_ref[...]

    reverse = (iota((taps, 2 * taps), 0) + iota((taps, 2 * taps), 1) == taps).astype(BF16)
    short_base = dot(filters, reverse)
    wide = span + taps
    place = iota((1, wide), 1)
    lag = jnp.where(place <= rows, rows - place, rows + wide - place)
    zero = jnp.logical_and(place > rows, place <= span)
    modal = residue * jnp.exp(-rate * lag.astype(F32))
    modal = jnp.where(zero, 0.0, modal)
    long_base = jnp.sum(modal.reshape(TILE_GROUPS, modes, wide), axis=1)

    for s in range(samples):
        product_window[s, :, :taps] = jnp.zeros((LANES, taps), BF16)
        mixed_window[s, :, :before] = jnp.zeros((LANES, before), BF16)
        border = border_ref[s * taps : (s + 1) * taps, :].astype(F32)
        product_window[s, :, taps : 2 * taps] = border.T.astype(BF16)
        product = product_of(key_ref[s], value_ref[s]).astype(F32)
        product_window[s, :, 2 * taps :] = product.T.astype(BF16)

    skip = jnp.broadcast_to(skip_ref[...], (8, LANES)).T[:, :1]
    for g in range(TILE_GROUPS):
        channels = slice(g * GROUP, (g + 1) * GROUP)
        spread = jnp.broadcast_to(short_base[g : g + 1], (taps, 2 * taps))
        short_table = pltpu.roll(spread, 0, 1, stride=1, stride_axis=0).astype(BF16)
        pieces = [
            product_window[s, channels, b * taps : (b + 2) * taps]
            for s in range(samples)
            for b in range(blocks + 1)
        ]
        mixed = dot_rows(jnp.concatenate(pieces, axis=0), short_table).astype(BF16)
        for s in range(samples):
            for b in range(blocks + 1):
                first = (s * (blocks + 1) + b) * GROUP
                mixed_window[s, channels, before + b * taps : before + (b + 1) * taps] = mixed[
                    first : first + GROUP
                ]
        spread = jnp.broadcast_to(long_base[g : g + 1], (taps, wide))
        long_table = pltpu.roll(spread, 0, 1, stride=1, stride_axis=0)[:, :span].astype(BF16)
        pieces = [
            mixed_window[s, channels, b * taps : b * taps + span]
            for s in range(samples)
            for b in range(blocks)
        ]
        filtered = dot_rows(jnp.concatenate(pieces, axis=0), long_table)
        for s in range(samples):
            for b in range(blocks):
                first = (s * blocks + b) * GROUP
                at = (s * (blocks + 1) + b + 1) * GROUP
                turned[s, channels, b * taps : (b + 1) * taps] = filtered[
                    first : first + GROUP
                ] + skip[channels] * mixed[at : at + GROUP].astype(F32)
    for s in range(samples):
        base_ref[s * rows : (s + 1) * rows, :] = turned[s].T.astype(BF16)

    tap_weights = jnp.exp(-rate * (taps - iota((1, taps), 1, F32)))
    spread = jnp.broadcast_to(
        filters.astype(F32)[:, None, :], (TILE_GROUPS, modes, taps)
    ).reshape(TILE_GROUPS * modes, taps)
    gain = residue * jnp.sum(spread * tap_weights, axis=1, keepdims=True)
    square = (TILE_GROUPS * modes, LANES)
    decay = own_group(jnp.broadcast_to(jnp.exp(-rate * float(rows - taps)), square), modes)
    gain = own_group(jnp.broadcast_to(gain, square), modes)
    first, state_rows = samples * taps, samples * modes
    early = border_ref[first : first + state_rows, :].astype(F32)
    early = early + border_ref[first + state_rows :, :].astype(F32)
    factors = jnp.concatenate([decay, gain, early], axis=0)
    base_ref[samples * rows :, :] = jnp.concatenate(halves(factors), axis=0)


def embed_kernel(token_ref, table_ref, out_ref):
    samples, rows = token_ref.shape
    vocab = table_ref.shape[0]
    for s in range(samples):
        ids = jnp.broadcast_to(token_ref[s : s + 1, :].astype(F32), (8, rows)).T[:, :1]
        one_hot = (ids == iota((rows, vocab), 1, F32)).astype(BF16)
        out_ref[s] = dot(one_hot, table_ref[...]).astype(BF16)


def gate_kernel(
    far_ref, own_ref, rate_ref, base_ref, query_ref, gated_ref, sum_ref, squares
):
    samples, rows, width = query_ref.shape
    height = (base_ref.shape[0] - samples * rows) // 2
    modes = own_ref.shape[0] // samples
    copies = sum_ref.shape[0]
    own = iota((LANES, LANES), 0) // modes == iota((LANES, LANES), 1) // GROUP
    for tile in range(width // LANES):
        lanes = slice(tile * LANES, (tile + 1) * LANES)
        rate = rate_ref[:, lanes]
        head = jnp.exp(-rate * (1.0 + iota((LANES, 1), 0, F32)))
        step = jnp.exp(-rate * float(LANES))
        after = [head]
        for _ in range(rows // LANES - 1):
            after.append(after[-1] * step)
        upper, lower = halves(jnp.concatenate(after, axis=0))
        after = jnp.concatenate([upper, lower, upper], axis=1)
        factors = base_ref[samples * rows :, lanes].astype(F32)
        factors = factors[:height] + factors[height:]
        for s in range(samples):
            carried = own_ref[s * modes : (s + 1) * modes, lanes]
            for first in range(s * modes, far_ref.shape[0], samples * modes):
                carried = carried + far_ref[first : first + modes, lanes].astype(F32)
            early = factors[(s + 2) * modes : (s + 3) * modes]
            state = (factors[:modes] * carried + early) * factors[modes : 2 * modes]
            spread = jnp.concatenate([state] * TILE_GROUPS, axis=0)
            upper, lower = halves(jnp.where(own, spread, 0.0))
            carry = dot(after, jnp.concatenate([upper, upper, lower], axis=0))
            base = base_ref[s * rows : (s + 1) * rows, lanes].astype(F32)
            gated = query_ref[s, :, lanes].astype(F32) * (base + carry)
            gated_ref[s, :, lanes] = gated
            if tile == 0:
                squares[s] = gated * gated
            else:
                squares[s] = squares[s] + gated * gated
    for s in range(samples):
        total = jnp.sum(squares[s].T, axis=0, keepdims=True)
        sum_ref[:, :, s * rows : (s + 1) * rows] = jnp.broadcast_to(
            total.reshape(1, 1, rows), (copies, 1, rows)
        )


def norm_kernel(
    length_ref, index_ref, sum_ref, gated_ref, embed_ref, gain_ref, out_target, out_ref, left, *, full
):
    samples, rows, _ = gated_ref.shape
    here = 128
    total = jnp.sum(sum_ref[...], axis=0)
    scale = jnp.broadcast_to(lax.rsqrt(total / full + 1e-06), (8, samples * rows)).T[:, :1]
    stores = []
    for s in range(samples):
        for part in range(rows // here):
            at = slice(part * here, (part + 1) * here)
            start = index_ref[0] * rows + part * here
            valid = start + iota((here, 1), 0) < length_ref[s]
            first = s * rows + part * here
            value = gated_ref[s, at, :] * scale[first : first + here] * gain_ref[...]
            value = value + embed_ref[s, at, :].astype(F32)
            out_ref[s, at, :] = jnp.where(valid, value, 0.0).astype(BF16)
            store = pltpu.make_async_copy(
                out_ref.at[s, at, :], out_target.at[s, at, :], left.at[s, part]
            )
            store.start()
            stores.append(store)
    for store in stores:
        store.wait()


def params(mebibytes):
    return pltpu.CompilerParams(vmem_limit_bytes=int(mebibytes * (1 << 20)))


def per_device(
    token_ids,
    lengths,
    embedding,
    query_act,
    key_act,
    value_act,
    short_filter,
    decay_rates,
    residues,
    skip_gain,
    norm_gain,
):
    samples, rows, width = query_act.shape
    taps = short_filter.shape[1]
    groups, modes = decay_rates.shape
    vocab = embedding.shape[0]
    chunks = lax.axis_size("ctx")
    columns = lax.axis_size("tp")
    index = lax.axis_index("ctx").reshape(1)
    tiles = width // LANES
    smem = pl.BlockSpec(memory_space=pltpu.SMEM)

    def cube():
        return pl.BlockSpec((samples, rows, LANES), lambda i: (0, 0, i))

    def flat(height):
        return pl.BlockSpec((height, LANES), lambda i: (0, i))

    def grouped(cols):
        return pl.BlockSpec((TILE_GROUPS, cols), lambda i: (i, 0))

    state_rows = samples * modes
    border_rows = samples * taps + 2 * state_rows
    base_rows = samples * rows + 2 * (2 * modes + state_rows)
    shape = jax.ShapeDtypeStruct
    whole = pl.BlockSpec((modes, groups), lambda i: (0, 0))
    rates = decay_rates.T
    near = 8 if chunks % 16 == 0 else 2
    far = chunks // near
    near_groups = [[g * near + i for i in range(near)] for g in range(far)]
    far_groups = [[g * near + i for g in range(far)] for i in range(near)]

    def exchange(blocks, groups):
        return lax.all_to_all(
            blocks, "ctx", split_axis=0, concat_axis=0, axis_index_groups=groups, tiled=True
        )


    vmem = pl.BlockSpec(memory_space=pltpu.VMEM)
    anywhere = pl.BlockSpec(memory_space=pl.ANY)

    def states_step(*refs):
        states_kernel(*refs, taps=taps)

    states, border = pl.pallas_call(
        states_step,
        in_specs=[anywhere, anywhere, anywhere],
        out_specs=[anywhere, anywhere],
        out_shape=[
            shape((near * state_rows, width), BF16),
            shape((border_rows, width), BF16),
        ],
        scratch_shapes=[
            pltpu.VMEM((modes, groups), F32),
            pltpu.VMEM((samples, rows, width), BF16),
            pltpu.VMEM((samples, rows, width), BF16),
            pltpu.VMEM((near * state_rows, width), BF16),
            pltpu.VMEM((border_rows, width), BF16),
            pltpu.SemaphoreType.DMA((1,)),
            pltpu.SemaphoreType.DMA((2, tiles)),
            pltpu.SemaphoreType.DMA((2, tiles)),
        ],
        compiler_params=params(60),
        name="states",
    )(rates, key_act, value_act)
    before = lax.ppermute(border, "ctx", [(i, i + 1) for i in range(chunks - 1)])
    gathered = exchange(states, near_groups)

    embedded = pl.pallas_call(
        embed_kernel,
        out_shape=shape((samples, rows, width), BF16),
        cost_estimate=pl.CostEstimate(
            flops=2 * samples * rows * width * vocab, bytes_accessed=4 << 20, transcendentals=0
        ),
        compiler_params=params(16),
        name="embed",
    )(token_ids, embedding)

    base = pl.pallas_call(
        local_kernel,
        grid=(tiles,),
        in_specs=[flat(border_rows), cube(), cube(), grouped(taps), whole, whole, flat(1)],
        out_specs=flat(base_rows),
        out_shape=shape((base_rows, width), BF16),
        scratch_shapes=[
            pltpu.VMEM((samples, LANES, rows + 2 * taps), BF16),
            pltpu.VMEM((samples, LANES, 2 * rows), BF16),
            pltpu.VMEM((samples, LANES, rows), F32),
        ],
        cost_estimate=pl.CostEstimate(
            flops=12_000_000_000, bytes_accessed=8 << 20, transcendentals=1 << 20
        ),
        compiler_params=params(60),
        name="local",
    )(
        before,
        key_act,
        value_act,
        short_filter,
        rates,
        residues.T,
        skip_gain.reshape(1, width),
    )

    def group_step(*refs):
        group_kernel(*refs, near=near, rows=rows)

    sent, own = pl.pallas_call(
        group_step,
        in_specs=[smem, vmem, vmem],
        out_shape=[shape((far * state_rows, width), BF16), shape((state_rows, width), F32)],
        compiler_params=params(8),
        name="group",
    )(index, jnp.repeat(rates, GROUP, axis=1), gathered)
    carried = exchange(sent, far_groups)

    gated, sums = pl.pallas_call(
        gate_kernel,
        out_shape=[
            shape((samples, rows, width), F32),
            shape((columns, 1, samples * rows), F32),
        ],
        scratch_shapes=[
            pltpu.VMEM((samples, rows, LANES), F32),
        ],
        compiler_params=params(16),
        name="gate",
    )(carried, own, decay_rates.reshape(1, groups * modes), base, query_act)
    shares = lax.all_to_all(sums, "tp", split_axis=0, concat_axis=0, tiled=True)

    def norm(*refs):
        norm_kernel(*refs, full=float(columns * width))

    return pl.pallas_call(
        norm,
        in_specs=[smem, smem, vmem, vmem, vmem, vmem],
        out_specs=anywhere,
        out_shape=shape((samples, rows, width), BF16),
        scratch_shapes=[
            pltpu.VMEM((samples, rows, width), BF16),
            pltpu.SemaphoreType.DMA((samples, rows // 128)),
        ],
        compiler_params=params(16),
        name="norm",
    )(lengths, index, shares, gated, embedded, norm_gain.reshape(1, width))


def solution(mesh):
    placed = (
        P(None, "ctx"),
        P(),
        P(None, "tp"),
        P(None, "ctx", "tp"),
        P(None, "ctx", "tp"),
        P(None, "ctx", "tp"),
        P("tp", None),
        P("tp", None),
        P("tp", None),
        P("tp"),
        P("tp"),
    )
    return jax.shard_map(
        per_device, mesh=mesh, in_specs=placed, out_specs=P(None, "ctx", "tp"), check_vma=False
    )
```

```python
import jax
import jax.numpy as jnp
from jax import lax
from jax.experimental import pallas as pl
from jax.experimental.pallas import tpu as pltpu
from jax.sharding import PartitionSpec as P

GROUP = 16
LANES = 128
TILE_GROUPS = LANES // GROUP
F32 = jnp.float32
BF16 = jnp.bfloat16


def iota(shape, dim, dtype=jnp.int32):
    return lax.broadcasted_iota(jnp.int32, shape, dim).astype(dtype)


def own_group(stacked, rows):
    lane_group = iota((rows, LANES), 1) // GROUP
    picked = stacked[:rows]
    for g in range(1, TILE_GROUPS):
        picked = jnp.where(lane_group == g, stacked[g * rows : (g + 1) * rows], picked)
    return picked


def halves(values):
    upper = values.astype(BF16)
    return upper, (values - upper.astype(F32)).astype(BF16)


def dot(a, b):
    return jnp.dot(a, b, preferred_element_type=F32)


def tile_column(table, tile):
    modes, groups = table.shape
    parts = []
    for g in range(TILE_GROUPS):
        here = iota((modes, groups), 1) == tile * TILE_GROUPS + g
        parts.append(jnp.sum(jnp.where(here, table, 0.0), axis=1, keepdims=True))
    return jnp.concatenate(parts, axis=0)


def product_of(key, value):
    return (key.astype(F32) * value.astype(F32)).astype(BF16)


def states_kernel(
    rate_source,
    key_source,
    value_source,
    state_target,
    border_target,
    rate_ref,
    key_ref,
    value_ref,
    state_ref,
    border_ref,
    ready,
    arrived,
    left,
    *,
    taps,
):
    samples, rows, width = key_ref.shape
    modes = rate_ref.shape[0]
    tiles = [slice(first, first + LANES) for first in range(0, width, LANES)]
    rate_load = pltpu.make_async_copy(rate_source, rate_ref, ready.at[0])
    rate_load.start()
    loads, stores = [], []
    for tile, lanes in enumerate(tiles):
        pair = (
            pltpu.make_async_copy(
                key_source.at[:, :, lanes], key_ref.at[:, :, lanes], arrived.at[0, tile]
            ),
            pltpu.make_async_copy(
                value_source.at[:, :, lanes], value_ref.at[:, :, lanes], arrived.at[1, tile]
            ),
        )
        for load in pair:
            load.start()
        loads.append(pair)
    rate_load.wait()
    tables = []
    for tile in range(len(tiles)):
        groups = range(tile * TILE_GROUPS, (tile + 1) * TILE_GROUPS)
        rate = jnp.concatenate([rate_ref[:, g : g + 1] for g in groups], axis=0)
        weights = [jnp.exp(-rate * (taps - 1.0 - iota((1, taps), 1, F32)))]
        step = jnp.exp(-rate * float(taps))
        for _ in range(rows // taps - 1):
            weights.insert(0, weights[0] * step)
        tables.append(jnp.concatenate(halves(jnp.concatenate(weights, axis=1)), axis=0))
    for tile, lanes in enumerate(tiles):
        weights = tables[tile]
        half = weights.shape[0] // 2
        for load in loads[tile]:
            load.wait()
        for s in range(samples):
            product = product_of(key_ref[s, :, lanes], value_ref[s, :, lanes])
            full = dot(weights, product)
            state = own_group(full[:half] + full[half:], modes)
            state = state.astype(BF16)
            for copy in range(state_ref.shape[0] // (samples * modes)):
                at = (copy * samples + s) * modes
                state_ref[at : at + modes, lanes] = state
            border_ref[s * taps : (s + 1) * taps, lanes] = product[rows - taps :]
            early = dot(weights[:, taps:], product[: rows - taps])
            upper, lower = halves(own_group(early[:half] + early[half:], modes))
            first = samples * taps + s * modes
            border_ref[first : first + modes, lanes] = upper
            border_ref[first + samples * modes : first + (samples + 1) * modes, lanes] = lower
        pair = (
            pltpu.make_async_copy(
                state_ref.at[:, lanes], state_target.at[:, lanes], left.at[0, tile]
            ),
            pltpu.make_async_copy(
                border_ref.at[:, lanes], border_target.at[:, lanes], left.at[1, tile]
            ),
        )
        for store in pair:
            store.start()
            stores.append(store)
    for store in stores:
        store.wait()


def group_kernel(index_ref, rate_ref, state_ref, far_ref, own_ref, *, near, rows):
    height = own_ref.shape[0]
    far = far_ref.shape[0] // height
    modes = rate_ref.shape[0]
    group, place = index_ref[0] // near, lax.rem(index_ref[0], near)
    rate = jnp.concatenate([rate_ref[...]] * (height // modes), axis=0) * float(rows)
    decay = jnp.exp(-rate)
    held = jnp.zeros(own_ref.shape, F32)
    own, short = held, held
    for p in range(near):
        own = jnp.where(place == p + 1, held, own)
        short = held
        held = decay * held + state_ref[p * height : (p + 1) * height, :].astype(F32)
    own_ref[...] = own
    for other in range(far):
        ahead = (other - group) * near + place - near - 1
        weight = jnp.exp(-rate * jnp.maximum(ahead, 0).astype(F32))
        value = jnp.where(ahead < 0, short, weight * held)
        value = jnp.where(other > group, value, 0.0)
        far_ref[other * height : (other + 1) * height, :] = value.astype(BF16)


def dot_rows(a, b):
    return lax.dot_general(a, b, (((1,), (1,)), ((), ())), preferred_element_type=F32)


def local_kernel(
    border_ref,
    key_ref,
    value_ref,
    filter_ref,
    rate_ref,
    residue_ref,
    skip_ref,
    base_ref,
    product_window,
    mixed_window,
    turned,
):
    samples, rows, _ = key_ref.shape
    modes = rate_ref.shape[0]
    taps = filter_ref.shape[1]
    span = rows + taps
    blocks = rows // taps
    before = span - 2 * taps
    tile = pl.program_id(0)
    rate = tile_column(rate_ref[...], tile)
    residue = tile_column(residue_ref[...], tile)
    filters = filter_ref[...]

    reverse = (iota((taps, 2 * taps), 0) + iota((taps, 2 * taps), 1) == taps).astype(BF16)
    short_base = dot(filters, reverse)
    wide = span + taps
    place = iota((1, wide), 1)
    lag = jnp.where(place <= rows, rows - place, rows + wide - place)
    zero = jnp.logical_and(place > rows, place <= span)
    modal = residue * jnp.exp(-rate * lag.astype(F32))
    modal = jnp.where(zero, 0.0, modal)
    long_base = jnp.sum(modal.reshape(TILE_GROUPS, modes, wide), axis=1)

    for s in range(samples):
        product_window[s, :, :taps] = jnp.zeros((LANES, taps), BF16)
        mixed_window[s, :, :before] = jnp.zeros((LANES, before), BF16)
        border = border_ref[s * taps : (s + 1) * taps, :].astype(F32)
        product_window[s, :, taps : 2 * taps] = border.T.astype(BF16)
        product = product_of(key_ref[s], value_ref[s]).astype(F32)
        product_window[s, :, 2 * taps :] = product.T.astype(BF16)

    skip = jnp.broadcast_to(skip_ref[...], (8, LANES)).T[:, :1]
    for g in range(TILE_GROUPS):
        channels = slice(g * GROUP, (g + 1) * GROUP)
        spread = jnp.broadcast_to(short_base[g : g + 1], (taps, 2 * taps))
        short_table = pltpu.roll(spread, 0, 1, stride=1, stride_axis=0).astype(BF16)
        pieces = [
            product_window[s, channels, b * taps : (b + 2) * taps]
            for s in range(samples)
            for b in range(blocks + 1)
        ]
        mixed = dot_rows(jnp.concatenate(pieces, axis=0), short_table).astype(BF16)
        for s in range(samples):
            for b in range(blocks + 1):
                first = (s * (blocks + 1) + b) * GROUP
                mixed_window[s, channels, before + b * taps : before + (b + 1) * taps] = mixed[
                    first : first + GROUP
                ]
        spread = jnp.broadcast_to(long_base[g : g + 1], (taps, wide))
        long_table = pltpu.roll(spread, 0, 1, stride=1, stride_axis=0)[:, :span].astype(BF16)
        pieces = [
            mixed_window[s, channels, b * taps : b * taps + span]
            for s in range(samples)
            for b in range(blocks)
        ]
        filtered = dot_rows(jnp.concatenate(pieces, axis=0), long_table)
        for s in range(samples):
            for b in range(blocks):
                first = (s * blocks + b) * GROUP
                at = (s * (blocks + 1) + b + 1) * GROUP
                turned[s, channels, b * taps : (b + 1) * taps] = filtered[
                    first : first + GROUP
                ] + skip[channels] * mixed[at : at + GROUP].astype(F32)
    for s in range(samples):
        base_ref[s * rows : (s + 1) * rows, :] = turned[s].T.astype(BF16)

    tap_weights = jnp.exp(-rate * (taps - iota((1, taps), 1, F32)))
    spread = jnp.broadcast_to(
        filters.astype(F32)[:, None, :], (TILE_GROUPS, modes, taps)
    ).reshape(TILE_GROUPS * modes, taps)
    gain = residue * jnp.sum(spread * tap_weights, axis=1, keepdims=True)
    square = (TILE_GROUPS * modes, LANES)
    decay = own_group(jnp.broadcast_to(jnp.exp(-rate * float(rows - taps)), square), modes)
    gain = own_group(jnp.broadcast_to(gain, square), modes)
    first, state_rows = samples * taps, samples * modes
    early = border_ref[first : first + state_rows, :].astype(F32)
    early = early + border_ref[first + state_rows :, :].astype(F32)
    factors = jnp.concatenate([decay, gain, early], axis=0)
    base_ref[samples * rows :, :] = jnp.concatenate(halves(factors), axis=0)


def embed_kernel(token_ref, table_ref, out_ref):
    samples, rows = token_ref.shape
    vocab = table_ref.shape[0]
    for s in range(samples):
        ids = jnp.broadcast_to(token_ref[s : s + 1, :].astype(F32), (8, rows)).T[:, :1]
        one_hot = (ids == iota((rows, vocab), 1, F32)).astype(BF16)
        out_ref[s] = dot(one_hot, table_ref[...]).astype(BF16)


def gate_kernel(
    far_ref, own_ref, rate_ref, base_ref, query_ref, gated_ref, sum_ref, squares
):
    samples, rows, width = query_ref.shape
    height = (base_ref.shape[0] - samples * rows) // 2
    modes = own_ref.shape[0] // samples
    copies = sum_ref.shape[0]
    own = iota((LANES, LANES), 0) // modes == iota((LANES, LANES), 1) // GROUP
    for tile in range(width // LANES):
        lanes = slice(tile * LANES, (tile + 1) * LANES)
        rate = rate_ref[:, lanes]
        head = jnp.exp(-rate * (1.0 + iota((LANES, 1), 0, F32)))
        step = jnp.exp(-rate * float(LANES))
        after = [head]
        for _ in range(rows // LANES - 1):
            after.append(after[-1] * step)
        upper, lower = halves(jnp.concatenate(after, axis=0))
        after = jnp.concatenate([upper, lower, upper], axis=1)
        factors = base_ref[samples * rows :, lanes].astype(F32)
        factors = factors[:height] + factors[height:]
        for s in range(samples):
            carried = own_ref[s * modes : (s + 1) * modes, lanes]
            for first in range(s * modes, far_ref.shape[0], samples * modes):
                carried = carried + far_ref[first : first + modes, lanes].astype(F32)
            early = factors[(s + 2) * modes : (s + 3) * modes]
            state = (factors[:modes] * carried + early) * factors[modes : 2 * modes]
            spread = jnp.concatenate([state] * TILE_GROUPS, axis=0)
            upper, lower = halves(jnp.where(own, spread, 0.0))
            carry = dot(after, jnp.concatenate([upper, upper, lower], axis=0))
            base = base_ref[s * rows : (s + 1) * rows, lanes].astype(F32)
            gated = query_ref[s, :, lanes].astype(F32) * (base + carry)
            gated_ref[s, :, lanes] = gated
            if tile == 0:
                squares[s] = gated * gated
            else:
                squares[s] = squares[s] + gated * gated
    for s in range(samples):
        total = jnp.sum(squares[s].T, axis=0, keepdims=True)
        sum_ref[:, :, s * rows : (s + 1) * rows] = jnp.broadcast_to(
            total.reshape(1, 1, rows), (copies, 1, rows)
        )


def norm_kernel(
    length_ref, index_ref, sum_ref, gated_ref, embed_ref, gain_ref, out_target, out_ref, left, *, full
):
    samples, rows, _ = gated_ref.shape
    here = 128
    total = jnp.sum(sum_ref[...], axis=0)
    scale = jnp.broadcast_to(lax.rsqrt(total / full + 1e-06), (8, samples * rows)).T[:, :1]
    stores = []
    for s in range(samples):
        for part in range(rows // here):
            at = slice(part * here, (part + 1) * here)
            start = index_ref[0] * rows + part * here
            valid = start + iota((here, 1), 0) < length_ref[s]
            first = s * rows + part * here
            value = gated_ref[s, at, :] * scale[first : first + here] * gain_ref[...]
            value = value + embed_ref[s, at, :].astype(F32)
            out_ref[s, at, :] = jnp.where(valid, value, 0.0).astype(BF16)
            store = pltpu.make_async_copy(
                out_ref.at[s, at, :], out_target.at[s, at, :], left.at[s, part]
            )
            store.start()
            stores.append(store)
    for store in stores:
        store.wait()


def params(mebibytes):
    return pltpu.CompilerParams(vmem_limit_bytes=int(mebibytes * (1 << 20)))


def per_device(
    token_ids,
    lengths,
    embedding,
    query_act,
    key_act,
    value_act,
    short_filter,
    decay_rates,
    residues,
    skip_gain,
    norm_gain,
):
    samples, rows, width = query_act.shape
    taps = short_filter.shape[1]
    groups, modes = decay_rates.shape
    vocab = embedding.shape[0]
    chunks = lax.axis_size("ctx")
    columns = lax.axis_size("tp")
    index = lax.axis_index("ctx").reshape(1)
    tiles = width // LANES
    smem = pl.BlockSpec(memory_space=pltpu.SMEM)

    def cube():
        return pl.BlockSpec((samples, rows, LANES), lambda i: (0, 0, i))

    def flat(height):
        return pl.BlockSpec((height, LANES), lambda i: (0, i))

    def grouped(cols):
        return pl.BlockSpec((TILE_GROUPS, cols), lambda i: (i, 0))

    state_rows = samples * modes
    border_rows = samples * taps + 2 * state_rows
    base_rows = samples * rows + 2 * (2 * modes + state_rows)
    shape = jax.ShapeDtypeStruct
    whole = pl.BlockSpec((modes, groups), lambda i: (0, 0))
    rates = decay_rates.T
    near = 4 if chunks % 16 == 0 else 2
    far = chunks // near
    near_groups = [[g * near + i for i in range(near)] for g in range(far)]
    far_groups = [[g * near + i for g in range(far)] for i in range(near)]

    def exchange(blocks, groups):
        return lax.all_to_all(
            blocks, "ctx", split_axis=0, concat_axis=0, axis_index_groups=groups, tiled=True
        )


    vmem = pl.BlockSpec(memory_space=pltpu.VMEM)
    anywhere = pl.BlockSpec(memory_space=pl.ANY)

    def states_step(*refs):
        states_kernel(*refs, taps=taps)

    states, border = pl.pallas_call(
        states_step,
        in_specs=[anywhere, anywhere, anywhere],
        out_specs=[anywhere, anywhere],
        out_shape=[
            shape((near * state_rows, width), BF16),
            shape((border_rows, width), BF16),
        ],
        scratch_shapes=[
            pltpu.VMEM((modes, groups), F32),
            pltpu.VMEM((samples, rows, width), BF16),
            pltpu.VMEM((samples, rows, width), BF16),
            pltpu.VMEM((near * state_rows, width), BF16),
            pltpu.VMEM((border_rows, width), BF16),
            pltpu.SemaphoreType.DMA((1,)),
            pltpu.SemaphoreType.DMA((2, tiles)),
            pltpu.SemaphoreType.DMA((2, tiles)),
        ],
        compiler_params=params(60),
        name="states",
    )(rates, key_act, value_act)
    before = lax.ppermute(border, "ctx", [(i, i + 1) for i in range(chunks - 1)])
    gathered = exchange(states, near_groups)

    embedded = pl.pallas_call(
        embed_kernel,
        out_shape=shape((samples, rows, width), BF16),
        cost_estimate=pl.CostEstimate(
            flops=2 * samples * rows * width * vocab, bytes_accessed=4 << 20, transcendentals=0
        ),
        compiler_params=params(16),
        name="embed",
    )(token_ids, embedding)

    base = pl.pallas_call(
        local_kernel,
        grid=(tiles,),
        in_specs=[flat(border_rows), cube(), cube(), grouped(taps), whole, whole, flat(1)],
        out_specs=flat(base_rows),
        out_shape=shape((base_rows, width), BF16),
        scratch_shapes=[
            pltpu.VMEM((samples, LANES, rows + 2 * taps), BF16),
            pltpu.VMEM((samples, LANES, 2 * rows), BF16),
            pltpu.VMEM((samples, LANES, rows), F32),
        ],
        cost_estimate=pl.CostEstimate(
            flops=12_000_000_000, bytes_accessed=8 << 20, transcendentals=1 << 20
        ),
        compiler_params=params(60),
        name="local",
    )(
        before,
        key_act,
        value_act,
        short_filter,
        rates,
        residues.T,
        skip_gain.reshape(1, width),
    )

    def group_step(*refs):
        group_kernel(*refs, near=near, rows=rows)

    sent, own = pl.pallas_call(
        group_step,
        in_specs=[smem, vmem, vmem],
        out_shape=[shape((far * state_rows, width), BF16), shape((state_rows, width), F32)],
        compiler_params=params(8),
        name="group",
    )(index, jnp.repeat(rates, GROUP, axis=1), gathered)
    carried = exchange(sent, far_groups)

    gated, sums = pl.pallas_call(
        gate_kernel,
        out_shape=[
            shape((samples, rows, width), F32),
            shape((columns, 1, samples * rows), F32),
        ],
        scratch_shapes=[
            pltpu.VMEM((samples, rows, LANES), F32),
        ],
        compiler_params=params(16),
        name="gate",
    )(carried, own, decay_rates.reshape(1, groups * modes), base, query_act)
    shares = lax.all_to_all(sums, "tp", split_axis=0, concat_axis=0, tiled=True)

    def norm(*refs):
        norm_kernel(*refs, full=float(columns * width))

    return pl.pallas_call(
        norm,
        in_specs=[smem, smem, vmem, vmem, vmem, vmem],
        out_specs=anywhere,
        out_shape=shape((samples, rows, width), BF16),
        scratch_shapes=[
            pltpu.VMEM((samples, rows, width), BF16),
            pltpu.SemaphoreType.DMA((samples, rows // 128)),
        ],
        compiler_params=params(16),
        name="norm",
    )(lengths, index, shares, gated, embedded, norm_gain.reshape(1, width))


def solution(mesh):
    placed = (
        P(None, "ctx"),
        P(),
        P(None, "tp"),
        P(None, "ctx", "tp"),
        P(None, "ctx", "tp"),
        P(None, "ctx", "tp"),
        P("tp", None),
        P("tp", None),
        P("tp", None),
        P("tp"),
        P("tp"),
    )
    return jax.shard_map(
        per_device, mesh=mesh, in_specs=placed, out_specs=P(None, "ctx", "tp"), check_vma=False
    )
```

```python
import jax
import jax.numpy as jnp
from jax import lax
from jax.experimental import pallas as pl
from jax.experimental.pallas import tpu as pltpu
from jax.sharding import PartitionSpec as P

GROUP = 16
LANES = 128
TILE_GROUPS = LANES // GROUP
F32 = jnp.float32
BF16 = jnp.bfloat16


def iota(shape, dim, dtype=jnp.int32):
    return lax.broadcasted_iota(jnp.int32, shape, dim).astype(dtype)


def own_group(stacked, rows):
    lane_group = iota((rows, LANES), 1) // GROUP
    picked = stacked[:rows]
    for g in range(1, TILE_GROUPS):
        picked = jnp.where(lane_group == g, stacked[g * rows : (g + 1) * rows], picked)
    return picked


def halves(values):
    upper = values.astype(BF16)
    return upper, (values - upper.astype(F32)).astype(BF16)


def dot(a, b):
    return jnp.dot(a, b, preferred_element_type=F32)


def tile_column(table, tile):
    modes, groups = table.shape
    parts = []
    for g in range(TILE_GROUPS):
        here = iota((modes, groups), 1) == tile * TILE_GROUPS + g
        parts.append(jnp.sum(jnp.where(here, table, 0.0), axis=1, keepdims=True))
    return jnp.concatenate(parts, axis=0)


def product_of(key, value):
    return (key.astype(F32) * value.astype(F32)).astype(BF16)


def states_kernel(
    rate_source,
    key_source,
    value_source,
    state_target,
    border_target,
    rate_ref,
    key_ref,
    value_ref,
    state_ref,
    border_ref,
    ready,
    arrived,
    left,
    *,
    taps,
):
    samples, rows, width = key_ref.shape
    modes = rate_ref.shape[0]
    tiles = [slice(first, first + LANES) for first in range(0, width, LANES)]
    rate_load = pltpu.make_async_copy(rate_source, rate_ref, ready.at[0])
    rate_load.start()
    loads, stores = [], []
    for tile, lanes in enumerate(tiles):
        pair = (
            pltpu.make_async_copy(
                key_source.at[:, :, lanes], key_ref.at[:, :, lanes], arrived.at[0, tile]
            ),
            pltpu.make_async_copy(
                value_source.at[:, :, lanes], value_ref.at[:, :, lanes], arrived.at[1, tile]
            ),
        )
        for load in pair:
            load.start()
        loads.append(pair)
    rate_load.wait()
    tables = []
    for tile in range(len(tiles)):
        groups = range(tile * TILE_GROUPS, (tile + 1) * TILE_GROUPS)
        rate = jnp.concatenate([rate_ref[:, g : g + 1] for g in groups], axis=0)
        weights = [jnp.exp(-rate * (taps - 1.0 - iota((1, taps), 1, F32)))]
        step = jnp.exp(-rate * float(taps))
        for _ in range(rows // taps - 1):
            weights.insert(0, weights[0] * step)
        tables.append(jnp.concatenate(halves(jnp.concatenate(weights, axis=1)), axis=0))
    for tile, lanes in enumerate(tiles):
        weights = tables[tile]
        half = weights.shape[0] // 2
        for load in loads[tile]:
            load.wait()
        for s in range(samples):
            product = product_of(key_ref[s, :, lanes], value_ref[s, :, lanes])
            full = dot(weights, product)
            state = own_group(full[:half] + full[half:], modes)
            state = state.astype(BF16)
            for copy in range(state_ref.shape[0] // (samples * modes)):
                at = (copy * samples + s) * modes
                state_ref[at : at + modes, lanes] = state
            border_ref[s * taps : (s + 1) * taps, lanes] = product[rows - taps :]
            early = dot(weights[:, taps:], product[: rows - taps])
            upper, lower = halves(own_group(early[:half] + early[half:], modes))
            first = samples * taps + s * modes
            border_ref[first : first + modes, lanes] = upper
            border_ref[first + samples * modes : first + (samples + 1) * modes, lanes] = lower
        pair = (
            pltpu.make_async_copy(
                state_ref.at[:, lanes], state_target.at[:, lanes], left.at[0, tile]
            ),
            pltpu.make_async_copy(
                border_ref.at[:, lanes], border_target.at[:, lanes], left.at[1, tile]
            ),
        )
        for store in pair:
            store.start()
            stores.append(store)
    for store in stores:
        store.wait()


def group_kernel(index_ref, rate_ref, state_ref, near_ref, *, near, far, rows):
    height = near_ref.shape[0] // near
    modes = rate_ref.shape[0]
    group, place = index_ref[0] // near, lax.rem(index_ref[0], near)
    rate = jnp.concatenate([rate_ref[...]] * (height // modes), axis=0) * float(rows)
    stride = jnp.exp(-rate * float(near))
    held = jnp.zeros(rate.shape, F32)
    mine, past, short, last = held, held, held, held
    for g in range(far):
        state = state_ref[g * height : (g + 1) * height, :].astype(F32)
        mine = jnp.where(group == g, state, mine)
        past = jnp.where(group == g, held, past)
        short = jnp.where(group == g, last, short)
        last = held
        held = stride * held + state
    short = jnp.exp(-rate * (near - 1.0)) * short
    for other in range(near):
        ahead = other - place - 2
        weight = jnp.exp(-rate * jnp.maximum(ahead, 0).astype(F32))
        value = jnp.where(ahead >= 0, weight * mine, 0.0)
        weight = jnp.exp(-rate * jnp.maximum(ahead + near, 0).astype(F32))
        value = value + jnp.where(ahead + near >= 0, weight * past, short)
        near_ref[other * height : (other + 1) * height, :] = value.astype(BF16)


def dot_rows(a, b):
    return lax.dot_general(a, b, (((1,), (1,)), ((), ())), preferred_element_type=F32)


def local_kernel(
    index_ref,
    border_ref,
    key_ref,
    value_ref,
    filter_ref,
    rate_ref,
    residue_ref,
    skip_ref,
    base_ref,
    turn_ref,
    product_window,
    mixed_window,
    turned,
):
    samples, rows, _ = key_ref.shape
    modes = rate_ref.shape[0]
    taps = filter_ref.shape[1]
    span = rows + taps
    blocks = rows // taps
    before = span - 2 * taps
    tile = pl.program_id(0)
    rate = tile_column(rate_ref[...], tile)
    residue = tile_column(residue_ref[...], tile)
    filters = filter_ref[...]

    reverse = (iota((taps, 2 * taps), 0) + iota((taps, 2 * taps), 1) == taps).astype(BF16)
    short_base = dot(filters, reverse)
    wide = span + taps
    place = iota((1, wide), 1)
    lag = jnp.where(place <= rows, rows - place, rows + wide - place)
    zero = jnp.logical_and(place > rows, place <= span)
    modal = residue * jnp.exp(-rate * lag.astype(F32))
    modal = jnp.where(zero, 0.0, modal)
    long_base = jnp.sum(modal.reshape(TILE_GROUPS, modes, wide), axis=1)

    for s in range(samples):
        product_window[s, :, :taps] = jnp.zeros((LANES, taps), BF16)
        mixed_window[s, :, :before] = jnp.zeros((LANES, before), BF16)
        border = border_ref[s * taps : (s + 1) * taps, :].astype(F32)
        product_window[s, :, taps : 2 * taps] = border.T.astype(BF16)
        product = product_of(key_ref[s], value_ref[s]).astype(F32)
        product_window[s, :, 2 * taps :] = product.T.astype(BF16)

    skip = jnp.broadcast_to(skip_ref[...], (8, LANES)).T[:, :1]
    for g in range(TILE_GROUPS):
        channels = slice(g * GROUP, (g + 1) * GROUP)
        spread = jnp.broadcast_to(short_base[g : g + 1], (taps, 2 * taps))
        short_table = pltpu.roll(spread, 0, 1, stride=1, stride_axis=0).astype(BF16)
        pieces = [
            product_window[s, channels, b * taps : (b + 2) * taps]
            for s in range(samples)
            for b in range(blocks + 1)
        ]
        mixed = dot_rows(jnp.concatenate(pieces, axis=0), short_table).astype(BF16)
        for s in range(samples):
            for b in range(blocks + 1):
                first = (s * (blocks + 1) + b) * GROUP
                mixed_window[s, channels, before + b * taps : before + (b + 1) * taps] = mixed[
                    first : first + GROUP
                ]
        spread = jnp.broadcast_to(long_base[g : g + 1], (taps, wide))
        long_table = pltpu.roll(spread, 0, 1, stride=1, stride_axis=0)[:, :span].astype(BF16)
        pieces = [
            mixed_window[s, channels, b * taps : b * taps + span]
            for s in range(samples)
            for b in range(blocks)
        ]
        filtered = dot_rows(jnp.concatenate(pieces, axis=0), long_table)
        for s in range(samples):
            for b in range(blocks):
                first = (s * blocks + b) * GROUP
                at = (s * (blocks + 1) + b + 1) * GROUP
                turned[s, channels, b * taps : (b + 1) * taps] = filtered[
                    first : first + GROUP
                ] + skip[channels] * mixed[at : at + GROUP].astype(F32)
    for s in range(samples):
        base_ref[s * rows : (s + 1) * rows, :] = turned[s].T.astype(BF16)

    tap_weights = jnp.exp(-rate * (taps - iota((1, taps), 1, F32)))
    spread = jnp.broadcast_to(
        filters.astype(F32)[:, None, :], (TILE_GROUPS, modes, taps)
    ).reshape(TILE_GROUPS * modes, taps)
    gain = residue * jnp.sum(spread * tap_weights, axis=1, keepdims=True)
    square = (TILE_GROUPS * modes, LANES)
    decay = own_group(jnp.broadcast_to(jnp.exp(-rate * float(rows - taps)), square), modes)
    gain = own_group(jnp.broadcast_to(gain, square), modes)
    first, state_rows = samples * taps, samples * modes
    early = border_ref[first : first + state_rows, :].astype(F32)
    early = early + border_ref[first + state_rows :, :].astype(F32)
    factors = jnp.concatenate([decay, gain, early], axis=0)
    base_ref[samples * rows :, :] = jnp.concatenate(halves(factors), axis=0)
    turn_ref[0] = index_ref[0]


def embed_kernel(token_ref, table_ref, out_ref):
    samples, rows = token_ref.shape
    vocab = table_ref.shape[0]
    for s in range(samples):
        ids = jnp.broadcast_to(token_ref[s : s + 1, :].astype(F32), (8, rows)).T[:, :1]
        one_hot = (ids == iota((rows, vocab), 1, F32)).astype(BF16)
        out_ref[s] = dot(one_hot, table_ref[...]).astype(BF16)


def gate_kernel(
    part_ref, rate_ref, base_ref, query_ref, gated_ref, sum_ref, squares
):
    samples, rows, width = query_ref.shape
    height = (base_ref.shape[0] - samples * rows) // 2
    modes = height // (2 + samples)
    copies = sum_ref.shape[0]
    own = iota((LANES, LANES), 0) // modes == iota((LANES, LANES), 1) // GROUP
    for tile in range(width // LANES):
        lanes = slice(tile * LANES, (tile + 1) * LANES)
        rate = rate_ref[:, lanes]
        head = jnp.exp(-rate * (1.0 + iota((LANES, 1), 0, F32)))
        step = jnp.exp(-rate * float(LANES))
        after = [head]
        for _ in range(rows // LANES - 1):
            after.append(after[-1] * step)
        upper, lower = halves(jnp.concatenate(after, axis=0))
        after = jnp.concatenate([upper, lower, upper], axis=1)
        factors = base_ref[samples * rows :, lanes].astype(F32)
        factors = factors[:height] + factors[height:]
        for s in range(samples):
            carried = jnp.zeros((modes, LANES), F32)
            for first in range(s * modes, part_ref.shape[0], samples * modes):
                carried = carried + part_ref[first : first + modes, lanes].astype(F32)
            early = factors[(s + 2) * modes : (s + 3) * modes]
            state = (factors[:modes] * carried + early) * factors[modes : 2 * modes]
            spread = jnp.concatenate([state] * TILE_GROUPS, axis=0)
            upper, lower = halves(jnp.where(own, spread, 0.0))
            carry = dot(after, jnp.concatenate([upper, upper, lower], axis=0))
            base = base_ref[s * rows : (s + 1) * rows, lanes].astype(F32)
            gated = query_ref[s, :, lanes].astype(F32) * (base + carry)
            gated_ref[s, :, lanes] = gated
            if tile == 0:
                squares[s] = gated * gated
            else:
                squares[s] = squares[s] + gated * gated
    for s in range(samples):
        total = jnp.sum(squares[s].T, axis=0, keepdims=True)
        sum_ref[:, :, s * rows : (s + 1) * rows] = jnp.broadcast_to(
            total.reshape(1, 1, rows), (copies, 1, rows)
        )


def norm_kernel(
    length_ref, index_ref, sum_ref, gated_ref, embed_ref, gain_ref, out_target, out_ref, left, *, full
):
    samples, rows, _ = gated_ref.shape
    here = 128
    total = jnp.sum(sum_ref[...], axis=0)
    scale = jnp.broadcast_to(lax.rsqrt(total / full + 1e-06), (8, samples * rows)).T[:, :1]
    stores = []
    for s in range(samples):
        for part in range(rows // here):
            at = slice(part * here, (part + 1) * here)
            start = index_ref[0] * rows + part * here
            valid = start + iota((here, 1), 0) < length_ref[s]
            first = s * rows + part * here
            value = gated_ref[s, at, :] * scale[first : first + here] * gain_ref[...]
            value = value + embed_ref[s, at, :].astype(F32)
            out_ref[s, at, :] = jnp.where(valid, value, 0.0).astype(BF16)
            store = pltpu.make_async_copy(
                out_ref.at[s, at, :], out_target.at[s, at, :], left.at[s, part]
            )
            store.start()
            stores.append(store)
    for store in stores:
        store.wait()


def params(mebibytes):
    return pltpu.CompilerParams(vmem_limit_bytes=int(mebibytes * (1 << 20)))


def per_device(
    token_ids,
    lengths,
    embedding,
    query_act,
    key_act,
    value_act,
    short_filter,
    decay_rates,
    residues,
    skip_gain,
    norm_gain,
):
    samples, rows, width = query_act.shape
    taps = short_filter.shape[1]
    groups, modes = decay_rates.shape
    vocab = embedding.shape[0]
    chunks = lax.axis_size("ctx")
    columns = lax.axis_size("tp")
    index = lax.axis_index("ctx").reshape(1)
    tiles = width // LANES
    smem = pl.BlockSpec(memory_space=pltpu.SMEM)

    def cube():
        return pl.BlockSpec((samples, rows, LANES), lambda i: (0, 0, i))

    def flat(height):
        return pl.BlockSpec((height, LANES), lambda i: (0, i))

    def grouped(cols):
        return pl.BlockSpec((TILE_GROUPS, cols), lambda i: (i, 0))

    state_rows = samples * modes
    border_rows = samples * taps + 2 * state_rows
    base_rows = samples * rows + 2 * (2 * modes + state_rows)
    shape = jax.ShapeDtypeStruct
    whole = pl.BlockSpec((modes, groups), lambda i: (0, 0))
    rates = decay_rates.T
    near = 8 if chunks % 16 == 0 else 2
    far = chunks // near
    near_groups = [[g * near + i for i in range(near)] for g in range(far)]
    far_groups = [[g * near + i for g in range(far)] for i in range(near)]

    def exchange(blocks, groups):
        return lax.all_to_all(
            blocks, "ctx", split_axis=0, concat_axis=0, axis_index_groups=groups, tiled=True
        )


    vmem = pl.BlockSpec(memory_space=pltpu.VMEM)
    anywhere = pl.BlockSpec(memory_space=pl.ANY)

    def states_step(*refs):
        states_kernel(*refs, taps=taps)

    states, border = pl.pallas_call(
        states_step,
        in_specs=[anywhere, anywhere, anywhere],
        out_specs=[anywhere, anywhere],
        out_shape=[
            shape((far * state_rows, width), BF16),
            shape((border_rows, width), BF16),
        ],
        scratch_shapes=[
            pltpu.VMEM((modes, groups), F32),
            pltpu.VMEM((samples, rows, width), BF16),
            pltpu.VMEM((samples, rows, width), BF16),
            pltpu.VMEM((far * state_rows, width), BF16),
            pltpu.VMEM((border_rows, width), BF16),
            pltpu.SemaphoreType.DMA((1,)),
            pltpu.SemaphoreType.DMA((2, tiles)),
            pltpu.SemaphoreType.DMA((2, tiles)),
        ],
        compiler_params=params(60),
        name="states",
    )(rates, key_act, value_act)
    before = lax.ppermute(border, "ctx", [(i, i + 1) for i in range(chunks - 1)])
    gathered = exchange(states, far_groups)

    embedded = pl.pallas_call(
        embed_kernel,
        out_shape=shape((samples, rows, width), BF16),
        cost_estimate=pl.CostEstimate(
            flops=2 * samples * rows * width * vocab, bytes_accessed=4 << 20, transcendentals=0
        ),
        compiler_params=params(16),
        name="embed",
    )(token_ids, embedding)

    base, turn = pl.pallas_call(
        local_kernel,
        grid=(tiles,),
        in_specs=[smem, flat(border_rows), cube(), cube(), grouped(taps), whole, whole, flat(1)],
        out_specs=[flat(base_rows), smem],
        out_shape=[shape((base_rows, width), BF16), shape((1,), jnp.int32)],
        scratch_shapes=[
            pltpu.VMEM((samples, LANES, rows + 2 * taps), BF16),
            pltpu.VMEM((samples, LANES, 2 * rows), BF16),
            pltpu.VMEM((samples, LANES, rows), F32),
        ],
        cost_estimate=pl.CostEstimate(
            flops=12_000_000_000, bytes_accessed=8 << 20, transcendentals=1 << 20
        ),
        compiler_params=params(60),
        name="local",
    )(
        index,
        before,
        key_act,
        value_act,
        short_filter,
        rates,
        residues.T,
        skip_gain.reshape(1, width),
    )

    def group_step(*refs):
        group_kernel(*refs, near=near, far=far, rows=rows)

    sent = pl.pallas_call(
        group_step,
        in_specs=[smem, vmem, vmem],
        out_shape=shape((near * state_rows, width), BF16),
        compiler_params=params(8),
        name="group",
    )(turn, jnp.repeat(rates, GROUP, axis=1), gathered)
    carried = exchange(sent, near_groups)

    gated, sums = pl.pallas_call(
        gate_kernel,
        out_shape=[
            shape((samples, rows, width), F32),
            shape((columns, 1, samples * rows), F32),
        ],
        scratch_shapes=[
            pltpu.VMEM((samples, rows, LANES), F32),
        ],
        compiler_params=params(16),
        name="gate",
    )(carried, decay_rates.reshape(1, groups * modes), base, query_act)
    shares = lax.all_to_all(sums, "tp", split_axis=0, concat_axis=0, tiled=True)

    def norm(*refs):
        norm_kernel(*refs, full=float(columns * width))

    return pl.pallas_call(
        norm,
        in_specs=[smem, smem, vmem, vmem, vmem, vmem],
        out_specs=anywhere,
        out_shape=shape((samples, rows, width), BF16),
        scratch_shapes=[
            pltpu.VMEM((samples, rows, width), BF16),
            pltpu.SemaphoreType.DMA((samples, rows // 128)),
        ],
        compiler_params=params(16),
        name="norm",
    )(lengths, index, shares, gated, embedded, norm_gain.reshape(1, width))


def solution(mesh):
    placed = (
        P(None, "ctx"),
        P(),
        P(None, "tp"),
        P(None, "ctx", "tp"),
        P(None, "ctx", "tp"),
        P(None, "ctx", "tp"),
        P("tp", None),
        P("tp", None),
        P("tp", None),
        P("tp"),
        P("tp"),
    )
    return jax.shard_map(
        per_device, mesh=mesh, in_specs=placed, out_specs=P(None, "ctx", "tp"), check_vma=False
    )
```

```python
import jax
import jax.numpy as jnp
from jax import lax
from jax.experimental import pallas as pl
from jax.experimental.pallas import tpu as pltpu
from jax.sharding import PartitionSpec as P

GROUP = 16
LANES = 128
TILE_GROUPS = LANES // GROUP
AHEAD = 3
F32 = jnp.float32
BF16 = jnp.bfloat16


def iota(shape, dim, dtype=jnp.int32):
    return lax.broadcasted_iota(jnp.int32, shape, dim).astype(dtype)


def own_group(stacked, rows):
    lane_group = iota((rows, LANES), 1) // GROUP
    picked = stacked[:rows]
    for g in range(1, TILE_GROUPS):
        picked = jnp.where(lane_group == g, stacked[g * rows : (g + 1) * rows], picked)
    return picked


def halves(values):
    upper = values.astype(BF16)
    return upper, (values - upper.astype(F32)).astype(BF16)


def dot(a, b):
    return jnp.dot(a, b, preferred_element_type=F32)


def tile_column(table, tile):
    modes, groups = table.shape
    parts = []
    for g in range(TILE_GROUPS):
        here = iota((modes, groups), 1) == tile * TILE_GROUPS + g
        parts.append(jnp.sum(jnp.where(here, table, 0.0), axis=1, keepdims=True))
    return jnp.concatenate(parts, axis=0)


def product_of(key, value):
    return (key.astype(F32) * value.astype(F32)).astype(BF16)


def states_kernel(
    rate_source,
    key_source,
    value_source,
    state_target,
    border_target,
    rate_ref,
    key_ref,
    value_ref,
    state_ref,
    border_ref,
    ready,
    arrived,
    left,
    *,
    taps,
):
    samples, rows, width = key_ref.shape
    modes = rate_ref.shape[0]
    tiles = [slice(first, first + LANES) for first in range(0, width, LANES)]
    rate_load = pltpu.make_async_copy(rate_source, rate_ref, ready.at[0])
    rate_load.start()
    loads, stores = [], []
    for tile, lanes in enumerate(tiles):
        pair = (
            pltpu.make_async_copy(
                key_source.at[:, :, lanes], key_ref.at[:, :, lanes], arrived.at[0, tile]
            ),
            pltpu.make_async_copy(
                value_source.at[:, :, lanes], value_ref.at[:, :, lanes], arrived.at[1, tile]
            ),
        )
        loads.append(pair)
    for pair in loads[:AHEAD]:
        for load in pair:
            load.start()
    rate_load.wait()
    tables = []
    for tile in range(len(tiles)):
        groups = range(tile * TILE_GROUPS, (tile + 1) * TILE_GROUPS)
        rate = jnp.concatenate([rate_ref[:, g : g + 1] for g in groups], axis=0)
        weights = [jnp.exp(-rate * (taps - 1.0 - iota((1, taps), 1, F32)))]
        step = jnp.exp(-rate * float(taps))
        for _ in range(rows // taps - 1):
            weights.insert(0, weights[0] * step)
        tables.append(jnp.concatenate(halves(jnp.concatenate(weights, axis=1)), axis=0))
    for tile, lanes in enumerate(tiles):
        weights = tables[tile]
        half = weights.shape[0] // 2
        for load in loads[tile]:
            load.wait()
        for load in loads[tile + AHEAD] if tile + AHEAD < len(tiles) else ():
            load.start()
        for s in range(samples):
            product = product_of(key_ref[s, :, lanes], value_ref[s, :, lanes])
            full = dot(weights, product)
            state = own_group(full[:half] + full[half:], modes)
            state = state.astype(BF16)
            for copy in range(state_ref.shape[0] // (samples * modes)):
                at = (copy * samples + s) * modes
                state_ref[at : at + modes, lanes] = state
            border_ref[s * taps : (s + 1) * taps, lanes] = product[rows - taps :]
            early = dot(weights[:, taps:], product[: rows - taps])
            first = samples * taps + s * modes
            early = own_group(early[:half] + early[half:], modes)
            border_ref[first : first + modes, lanes] = early.astype(BF16)
        pair = (
            pltpu.make_async_copy(
                state_ref.at[:, lanes], state_target.at[:, lanes], left.at[0, tile]
            ),
            pltpu.make_async_copy(
                border_ref.at[:, lanes], border_target.at[:, lanes], left.at[1, tile]
            ),
        )
        for store in pair:
            store.start()
            stores.append(store)
    for store in stores:
        store.wait()


def group_kernel(index_ref, rate_ref, state_ref, far_ref, own_ref, *, near, rows):
    height = own_ref.shape[0]
    far = far_ref.shape[0] // height
    modes = rate_ref.shape[0]
    group, place = index_ref[0] // near, lax.rem(index_ref[0], near)
    rate = jnp.concatenate([rate_ref[...]] * (height // modes), axis=0) * float(rows)
    decay = jnp.exp(-rate)
    held = jnp.zeros(own_ref.shape, F32)
    own, short = held, held
    for p in range(near):
        own = jnp.where(place == p + 1, held, own)
        short = held
        held = decay * held + state_ref[p * height : (p + 1) * height, :].astype(F32)
    own_ref[...] = own
    for other in range(far):
        ahead = (other - group) * near + place - near - 1
        weight = jnp.exp(-rate * jnp.maximum(ahead, 0).astype(F32))
        value = jnp.where(ahead < 0, short, weight * held)
        value = jnp.where(other > group, value, 0.0)
        far_ref[other * height : (other + 1) * height, :] = value.astype(BF16)


def dot_rows(a, b):
    return lax.dot_general(a, b, (((1,), (1,)), ((), ())), preferred_element_type=F32)


def local_kernel(
    border_ref,
    key_ref,
    value_ref,
    filter_ref,
    rate_ref,
    residue_ref,
    skip_ref,
    base_ref,
    product_window,
    mixed_window,
    turned,
):
    samples, rows, _ = key_ref.shape
    modes = rate_ref.shape[0]
    taps = filter_ref.shape[1]
    span = rows + taps
    blocks = rows // taps
    before = span - 2 * taps
    tile = pl.program_id(0)
    rate = tile_column(rate_ref[...], tile)
    residue = tile_column(residue_ref[...], tile)
    filters = filter_ref[...]

    reverse = (iota((taps, 2 * taps), 0) + iota((taps, 2 * taps), 1) == taps).astype(BF16)
    short_base = dot(filters, reverse)
    wide = span + taps
    place = iota((1, wide), 1)
    lag = jnp.where(place <= rows, rows - place, rows + wide - place)
    zero = jnp.logical_and(place > rows, place <= span)
    modal = residue * jnp.exp(-rate * lag.astype(F32))
    modal = jnp.where(zero, 0.0, modal)
    long_base = jnp.sum(modal.reshape(TILE_GROUPS, modes, wide), axis=1)

    for s in range(samples):
        product_window[s, :, :taps] = jnp.zeros((LANES, taps), BF16)
        mixed_window[s, :, :before] = jnp.zeros((LANES, before), BF16)
        border = border_ref[s * taps : (s + 1) * taps, :].astype(F32)
        product_window[s, :, taps : 2 * taps] = border.T.astype(BF16)
        product = product_of(key_ref[s], value_ref[s]).astype(F32)
        product_window[s, :, 2 * taps :] = product.T.astype(BF16)

    skip = jnp.broadcast_to(skip_ref[...], (8, LANES)).T[:, :1]
    for g in range(TILE_GROUPS):
        channels = slice(g * GROUP, (g + 1) * GROUP)
        spread = jnp.broadcast_to(short_base[g : g + 1], (taps, 2 * taps))
        short_table = pltpu.roll(spread, 0, 1, stride=1, stride_axis=0).astype(BF16)
        pieces = [
            product_window[s, channels, b * taps : (b + 2) * taps]
            for s in range(samples)
            for b in range(blocks + 1)
        ]
        mixed = dot_rows(jnp.concatenate(pieces, axis=0), short_table).astype(BF16)
        for s in range(samples):
            for b in range(blocks + 1):
                first = (s * (blocks + 1) + b) * GROUP
                mixed_window[s, channels, before + b * taps : before + (b + 1) * taps] = mixed[
                    first : first + GROUP
                ]
        spread = jnp.broadcast_to(long_base[g : g + 1], (taps, wide))
        long_table = pltpu.roll(spread, 0, 1, stride=1, stride_axis=0)[:, :span].astype(BF16)
        pieces = [
            mixed_window[s, channels, b * taps : b * taps + span]
            for s in range(samples)
            for b in range(blocks)
        ]
        filtered = dot_rows(jnp.concatenate(pieces, axis=0), long_table)
        for s in range(samples):
            for b in range(blocks):
                first = (s * blocks + b) * GROUP
                at = (s * (blocks + 1) + b + 1) * GROUP
                turned[s, channels, b * taps : (b + 1) * taps] = filtered[
                    first : first + GROUP
                ] + skip[channels] * mixed[at : at + GROUP].astype(F32)
    for s in range(samples):
        base_ref[s * rows : (s + 1) * rows, :] = turned[s].T.astype(BF16)

    tap_weights = jnp.exp(-rate * (taps - iota((1, taps), 1, F32)))
    spread = jnp.broadcast_to(
        filters.astype(F32)[:, None, :], (TILE_GROUPS, modes, taps)
    ).reshape(TILE_GROUPS * modes, taps)
    gain = residue * jnp.sum(spread * tap_weights, axis=1, keepdims=True)
    square = (TILE_GROUPS * modes, LANES)
    decay = own_group(jnp.broadcast_to(jnp.exp(-rate * float(rows - taps)), square), modes)
    gain = own_group(jnp.broadcast_to(gain, square), modes)
    early = border_ref[samples * taps :, :].astype(F32)
    factors = jnp.concatenate([decay, gain, early], axis=0)
    base_ref[samples * rows :, :] = jnp.concatenate(halves(factors), axis=0)


def embed_kernel(token_ref, table_ref, out_ref):
    samples, rows = token_ref.shape
    vocab = table_ref.shape[0]
    for s in range(samples):
        ids = jnp.broadcast_to(token_ref[s : s + 1, :].astype(F32), (8, rows)).T[:, :1]
        one_hot = (ids == iota((rows, vocab), 1, F32)).astype(BF16)
        out_ref[s] = dot(one_hot, table_ref[...]).astype(BF16)


def gate_kernel(
    far_ref, own_ref, rate_ref, base_ref, query_ref, gated_ref, sum_ref, squares
):
    samples, rows, width = query_ref.shape
    height = (base_ref.shape[0] - samples * rows) // 2
    modes = own_ref.shape[0] // samples
    copies = sum_ref.shape[0]
    own = iota((LANES, LANES), 0) // modes == iota((LANES, LANES), 1) // GROUP
    for tile in range(width // LANES):
        lanes = slice(tile * LANES, (tile + 1) * LANES)
        rate = rate_ref[:, lanes]
        head = jnp.exp(-rate * (1.0 + iota((LANES, 1), 0, F32)))
        step = jnp.exp(-rate * float(LANES))
        after = [head]
        for _ in range(rows // LANES - 1):
            after.append(after[-1] * step)
        upper, lower = halves(jnp.concatenate(after, axis=0))
        after = jnp.concatenate([upper, lower, upper], axis=1)
        factors = base_ref[samples * rows :, lanes].astype(F32)
        factors = factors[:height] + factors[height:]
        for s in range(samples):
            carried = own_ref[s * modes : (s + 1) * modes, lanes]
            for first in range(s * modes, far_ref.shape[0], samples * modes):
                carried = carried + far_ref[first : first + modes, lanes].astype(F32)
            early = factors[(s + 2) * modes : (s + 3) * modes]
            state = (factors[:modes] * carried + early) * factors[modes : 2 * modes]
            spread = jnp.concatenate([state] * TILE_GROUPS, axis=0)
            upper, lower = halves(jnp.where(own, spread, 0.0))
            carry = dot(after, jnp.concatenate([upper, upper, lower], axis=0))
            base = base_ref[s * rows : (s + 1) * rows, lanes].astype(F32)
            gated = query_ref[s, :, lanes].astype(F32) * (base + carry)
            gated_ref[s, :, lanes] = gated
            if tile == 0:
                squares[s] = gated * gated
            else:
                squares[s] = squares[s] + gated * gated
    for s in range(samples):
        total = jnp.sum(squares[s].T, axis=0, keepdims=True)
        sum_ref[:, :, s * rows : (s + 1) * rows] = jnp.broadcast_to(
            total.reshape(1, 1, rows), (copies, 1, rows)
        )


def norm_kernel(
    length_ref, index_ref, sum_ref, gated_ref, embed_ref, gain_ref, out_target, out_ref, left, *, full
):
    samples, rows, _ = gated_ref.shape
    here = 128
    total = jnp.sum(sum_ref[...], axis=0)
    scale = jnp.broadcast_to(lax.rsqrt(total / full + 1e-06), (8, samples * rows)).T[:, :1]
    stores = []
    for s in range(samples):
        for part in range(rows // here):
            at = slice(part * here, (part + 1) * here)
            start = index_ref[0] * rows + part * here
            valid = start + iota((here, 1), 0) < length_ref[s]
            first = s * rows + part * here
            value = gated_ref[s, at, :] * scale[first : first + here] * gain_ref[...]
            value = value + embed_ref[s, at, :].astype(F32)
            out_ref[s, at, :] = jnp.where(valid, value, 0.0).astype(BF16)
            store = pltpu.make_async_copy(
                out_ref.at[s, at, :], out_target.at[s, at, :], left.at[s, part]
            )
            store.start()
            stores.append(store)
    for store in stores:
        store.wait()


def params(mebibytes):
    return pltpu.CompilerParams(vmem_limit_bytes=int(mebibytes * (1 << 20)))


def per_device(
    token_ids,
    lengths,
    embedding,
    query_act,
    key_act,
    value_act,
    short_filter,
    decay_rates,
    residues,
    skip_gain,
    norm_gain,
):
    samples, rows, width = query_act.shape
    taps = short_filter.shape[1]
    groups, modes = decay_rates.shape
    vocab = embedding.shape[0]
    chunks = lax.axis_size("ctx")
    columns = lax.axis_size("tp")
    index = lax.axis_index("ctx").reshape(1)
    tiles = width // LANES
    smem = pl.BlockSpec(memory_space=pltpu.SMEM)

    def cube():
        return pl.BlockSpec((samples, rows, LANES), lambda i: (0, 0, i))

    def flat(height):
        return pl.BlockSpec((height, LANES), lambda i: (0, i))

    def grouped(cols):
        return pl.BlockSpec((TILE_GROUPS, cols), lambda i: (i, 0))

    state_rows = samples * modes
    border_rows = samples * taps + state_rows
    base_rows = samples * rows + 2 * (2 * modes + state_rows)
    shape = jax.ShapeDtypeStruct
    whole = pl.BlockSpec((modes, groups), lambda i: (0, 0))
    rates = decay_rates.T
    near = 8 if chunks % 16 == 0 else 2
    far = chunks // near
    near_groups = [[g * near + i for i in range(near)] for g in range(far)]
    far_groups = [[g * near + i for g in range(far)] for i in range(near)]

    def exchange(blocks, groups):
        return lax.all_to_all(
            blocks, "ctx", split_axis=0, concat_axis=0, axis_index_groups=groups, tiled=True
        )


    vmem = pl.BlockSpec(memory_space=pltpu.VMEM)
    anywhere = pl.BlockSpec(memory_space=pl.ANY)

    def states_step(*refs):
        states_kernel(*refs, taps=taps)

    states, border = pl.pallas_call(
        states_step,
        in_specs=[anywhere, anywhere, anywhere],
        out_specs=[anywhere, anywhere],
        out_shape=[
            shape((near * state_rows, width), BF16),
            shape((border_rows, width), BF16),
        ],
        scratch_shapes=[
            pltpu.VMEM((modes, groups), F32),
            pltpu.VMEM((samples, rows, width), BF16),
            pltpu.VMEM((samples, rows, width), BF16),
            pltpu.VMEM((near * state_rows, width), BF16),
            pltpu.VMEM((border_rows, width), BF16),
            pltpu.SemaphoreType.DMA((1,)),
            pltpu.SemaphoreType.DMA((2, tiles)),
            pltpu.SemaphoreType.DMA((2, tiles)),
        ],
        compiler_params=params(60),
        name="states",
    )(rates, key_act, value_act)
    before = lax.ppermute(border, "ctx", [(i, i + 1) for i in range(chunks - 1)])
    gathered = exchange(states, near_groups)

    embedded = pl.pallas_call(
        embed_kernel,
        out_shape=shape((samples, rows, width), BF16),
        cost_estimate=pl.CostEstimate(
            flops=2 * samples * rows * width * vocab, bytes_accessed=4 << 20, transcendentals=0
        ),
        compiler_params=params(16),
        name="embed",
    )(token_ids, embedding)

    base = pl.pallas_call(
        local_kernel,
        grid=(tiles,),
        in_specs=[flat(border_rows), cube(), cube(), grouped(taps), whole, whole, flat(1)],
        out_specs=flat(base_rows),
        out_shape=shape((base_rows, width), BF16),
        scratch_shapes=[
            pltpu.VMEM((samples, LANES, rows + 2 * taps), BF16),
            pltpu.VMEM((samples, LANES, 2 * rows), BF16),
            pltpu.VMEM((samples, LANES, rows), F32),
        ],
        cost_estimate=pl.CostEstimate(
            flops=12_000_000_000, bytes_accessed=8 << 20, transcendentals=1 << 20
        ),
        compiler_params=params(60),
        name="local",
    )(
        before,
        key_act,
        value_act,
        short_filter,
        rates,
        residues.T,
        skip_gain.reshape(1, width),
    )

    def group_step(*refs):
        group_kernel(*refs, near=near, rows=rows)

    sent, own = pl.pallas_call(
        group_step,
        in_specs=[smem, vmem, vmem],
        out_shape=[shape((far * state_rows, width), BF16), shape((state_rows, width), F32)],
        compiler_params=params(8),
        name="group",
    )(index, jnp.repeat(rates, GROUP, axis=1), gathered)
    carried = exchange(sent, far_groups)

    gated, sums = pl.pallas_call(
        gate_kernel,
        out_shape=[
            shape((samples, rows, width), F32),
            shape((columns, 1, samples * rows), F32),
        ],
        scratch_shapes=[
            pltpu.VMEM((samples, rows, LANES), F32),
        ],
        compiler_params=params(16),
        name="gate",
    )(carried, own, decay_rates.reshape(1, groups * modes), base, query_act)
    shares = lax.all_to_all(sums, "tp", split_axis=0, concat_axis=0, tiled=True)

    def norm(*refs):
        norm_kernel(*refs, full=float(columns * width))

    return pl.pallas_call(
        norm,
        in_specs=[smem, smem, vmem, vmem, vmem, vmem],
        out_specs=anywhere,
        out_shape=shape((samples, rows, width), BF16),
        scratch_shapes=[
            pltpu.VMEM((samples, rows, width), BF16),
            pltpu.SemaphoreType.DMA((samples, rows // 128)),
        ],
        compiler_params=params(16),
        name="norm",
    )(lengths, index, shares, gated, embedded, norm_gain.reshape(1, width))


def solution(mesh):
    placed = (
        P(None, "ctx"),
        P(),
        P(None, "tp"),
        P(None, "ctx", "tp"),
        P(None, "ctx", "tp"),
        P(None, "ctx", "tp"),
        P("tp", None),
        P("tp", None),
        P("tp", None),
        P("tp"),
        P("tp"),
    )
    return jax.shard_map(
        per_device, mesh=mesh, in_specs=placed, out_specs=P(None, "ctx", "tp"), check_vma=False
    )
```

```python
import jax
import jax.numpy as jnp
from jax import lax
from jax.experimental import pallas as pl
from jax.experimental.pallas import tpu as pltpu
from jax.sharding import PartitionSpec as P

GROUP = 16
LANES = 128
TILE_GROUPS = LANES // GROUP
F32 = jnp.float32
BF16 = jnp.bfloat16


def iota(shape, dim, dtype=jnp.int32):
    return lax.broadcasted_iota(jnp.int32, shape, dim).astype(dtype)


def own_group(stacked, rows):
    lane_group = iota((rows, LANES), 1) // GROUP
    picked = stacked[:rows]
    for g in range(1, TILE_GROUPS):
        picked = jnp.where(lane_group == g, stacked[g * rows : (g + 1) * rows], picked)
    return picked


def halves(values):
    upper = values.astype(BF16)
    return upper, (values - upper.astype(F32)).astype(BF16)


def dot(a, b):
    return jnp.dot(a, b, preferred_element_type=F32)


def tile_column(table, tile):
    modes, groups = table.shape
    parts = []
    for g in range(TILE_GROUPS):
        here = iota((modes, groups), 1) == tile * TILE_GROUPS + g
        parts.append(jnp.sum(jnp.where(here, table, 0.0), axis=1, keepdims=True))
    return jnp.concatenate(parts, axis=0)


def product_of(key, value):
    return (key.astype(F32) * value.astype(F32)).astype(BF16)


def states_kernel(
    rate_source,
    key_source,
    value_source,
    state_target,
    border_target,
    rate_ref,
    key_ref,
    value_ref,
    state_ref,
    border_ref,
    ready,
    arrived,
    left,
    *,
    taps,
):
    samples, rows, width = key_ref.shape
    modes = rate_ref.shape[0]
    tiles = [slice(first, first + LANES) for first in range(0, width, LANES)]
    rate_load = pltpu.make_async_copy(rate_source, rate_ref, ready.at[0])
    rate_load.start()
    loads, stores = [], []
    for tile, lanes in enumerate(tiles):
        pair = (
            pltpu.make_async_copy(
                key_source.at[:, :, lanes], key_ref.at[:, :, lanes], arrived.at[0, tile]
            ),
            pltpu.make_async_copy(
                value_source.at[:, :, lanes], value_ref.at[:, :, lanes], arrived.at[1, tile]
            ),
        )
        for load in pair:
            load.start()
        loads.append(pair)
    rate_load.wait()
    tables = []
    for tile in range(len(tiles)):
        groups = range(tile * TILE_GROUPS, (tile + 1) * TILE_GROUPS)
        rate = jnp.concatenate([rate_ref[:, g : g + 1] for g in groups], axis=0)
        weights = [jnp.exp(-rate * (taps - 1.0 - iota((1, taps), 1, F32)))]
        step = jnp.exp(-rate * float(taps))
        for _ in range(rows // taps - 1):
            weights.insert(0, weights[0] * step)
        tables.append(jnp.concatenate(halves(jnp.concatenate(weights, axis=1)), axis=0))
    for tile, lanes in enumerate(tiles):
        weights = tables[tile]
        half = weights.shape[0] // 2
        for load in loads[tile]:
            load.wait()
        for s in range(samples):
            product = product_of(key_ref[s, :, lanes], value_ref[s, :, lanes])
            full = dot(weights, product)
            state = own_group(full[:half] + full[half:], modes)
            state = state.astype(BF16)
            for copy in range(state_ref.shape[0] // (samples * modes)):
                at = (copy * samples + s) * modes
                state_ref[at : at + modes, lanes] = state
            border_ref[s * taps : (s + 1) * taps, lanes] = product[rows - taps :]
            early = dot(weights[:, taps:], product[: rows - taps])
            upper, lower = halves(own_group(early[:half] + early[half:], modes))
            first = samples * taps + s * modes
            border_ref[first : first + modes, lanes] = upper
            border_ref[first + samples * modes : first + (samples + 1) * modes, lanes] = lower
        pair = (
            pltpu.make_async_copy(
                state_ref.at[:, lanes], state_target.at[:, lanes], left.at[0, tile]
            ),
            pltpu.make_async_copy(
                border_ref.at[:, lanes], border_target.at[:, lanes], left.at[1, tile]
            ),
        )
        for store in pair:
            store.start()
            stores.append(store)
    for store in stores:
        store.wait()


def group_kernel(index_ref, rate_ref, state_ref, far_ref, own_ref, *, near, rows):
    height = own_ref.shape[0]
    far = far_ref.shape[0] // height
    modes = rate_ref.shape[0]
    group, place = index_ref[0] // near, lax.rem(index_ref[0], near)
    rate = jnp.concatenate([rate_ref[...]] * (height // modes), axis=0) * float(rows)
    decay = jnp.exp(-rate)
    held = jnp.zeros(own_ref.shape, F32)
    own, short = held, held
    for p in range(near):
        own = jnp.where(place == p + 1, held, own)
        short = held
        held = decay * held + state_ref[p * height : (p + 1) * height, :].astype(F32)
    own_ref[...] = own
    for other in range(far):
        ahead = (other - group) * near + place - near - 1
        weight = jnp.exp(-rate * jnp.maximum(ahead, 0).astype(F32))
        value = jnp.where(ahead < 0, short, weight * held)
        value = jnp.where(other > group, value, 0.0)
        far_ref[other * height : (other + 1) * height, :] = value.astype(BF16)


def dot_rows(a, b):
    return lax.dot_general(a, b, (((1,), (1,)), ((), ())), preferred_element_type=F32)


def local_kernel(
    border_ref,
    key_ref,
    value_ref,
    filter_ref,
    rate_ref,
    residue_ref,
    skip_ref,
    base_ref,
    product_window,
    mixed_window,
    turned,
):
    samples, rows, _ = key_ref.shape
    modes = rate_ref.shape[0]
    taps = filter_ref.shape[1]
    span = rows + taps
    blocks = rows // taps
    before = span - 2 * taps
    tile = pl.program_id(0)
    rate = tile_column(rate_ref[...], tile)
    residue = tile_column(residue_ref[...], tile)
    filters = filter_ref[...]

    reverse = (iota((taps, 2 * taps), 0) + iota((taps, 2 * taps), 1) == taps).astype(BF16)
    short_base = dot(filters, reverse)
    wide = span + taps
    place = iota((1, wide), 1)
    lag = jnp.where(place <= rows, rows - place, rows + wide - place)
    zero = jnp.logical_and(place > rows, place <= span)
    modal = residue * jnp.exp(-rate * lag.astype(F32))
    modal = jnp.where(zero, 0.0, modal)
    long_base = jnp.sum(modal.reshape(TILE_GROUPS, modes, wide), axis=1)

    for s in range(samples):
        product_window[s, :, :taps] = jnp.zeros((LANES, taps), BF16)
        mixed_window[s, :, :before] = jnp.zeros((LANES, before), BF16)
        border = border_ref[s * taps : (s + 1) * taps, :].astype(F32)
        product_window[s, :, taps : 2 * taps] = border.T.astype(BF16)
        product = product_of(key_ref[s], value_ref[s]).astype(F32)
        product_window[s, :, 2 * taps :] = product.T.astype(BF16)

    skip = jnp.broadcast_to(skip_ref[...], (8, LANES)).T[:, :1]
    for g in range(TILE_GROUPS):
        channels = slice(g * GROUP, (g + 1) * GROUP)
        spread = jnp.broadcast_to(short_base[g : g + 1], (taps, 2 * taps))
        short_table = pltpu.roll(spread, 0, 1, stride=1, stride_axis=0).astype(BF16)
        pieces = [
            product_window[s, channels, b * taps : (b + 2) * taps]
            for s in range(samples)
            for b in range(blocks + 1)
        ]
        mixed = dot_rows(jnp.concatenate(pieces, axis=0), short_table).astype(BF16)
        for s in range(samples):
            for b in range(blocks + 1):
                first = (s * (blocks + 1) + b) * GROUP
                mixed_window[s, channels, before + b * taps : before + (b + 1) * taps] = mixed[
                    first : first + GROUP
                ]
        spread = jnp.broadcast_to(long_base[g : g + 1], (taps, wide))
        long_table = pltpu.roll(spread, 0, 1, stride=1, stride_axis=0)[:, :span].astype(BF16)
        pieces = [
            mixed_window[s, channels, b * taps : b * taps + span]
            for s in range(samples)
            for b in range(blocks)
        ]
        filtered = dot_rows(jnp.concatenate(pieces, axis=0), long_table)
        for s in range(samples):
            for b in range(blocks):
                first = (s * blocks + b) * GROUP
                at = (s * (blocks + 1) + b + 1) * GROUP
                turned[s, channels, b * taps : (b + 1) * taps] = filtered[
                    first : first + GROUP
                ] + skip[channels] * mixed[at : at + GROUP].astype(F32)
    for s in range(samples):
        base_ref[s * rows : (s + 1) * rows, :] = turned[s].T.astype(BF16)

    tap_weights = jnp.exp(-rate * (taps - iota((1, taps), 1, F32)))
    spread = jnp.broadcast_to(
        filters.astype(F32)[:, None, :], (TILE_GROUPS, modes, taps)
    ).reshape(TILE_GROUPS * modes, taps)
    gain = residue * jnp.sum(spread * tap_weights, axis=1, keepdims=True)
    square = (TILE_GROUPS * modes, LANES)
    decay = own_group(jnp.broadcast_to(jnp.exp(-rate * float(rows - taps)), square), modes)
    gain = own_group(jnp.broadcast_to(gain, square), modes)
    first, state_rows = samples * taps, samples * modes
    early = border_ref[first : first + state_rows, :].astype(F32)
    early = early + border_ref[first + state_rows :, :].astype(F32)
    factors = jnp.concatenate([decay, gain, early], axis=0)
    base_ref[samples * rows :, :] = jnp.concatenate(halves(factors), axis=0)


def embed_kernel(token_ref, table_ref, out_ref):
    samples, rows = token_ref.shape
    vocab = table_ref.shape[0]
    for s in range(samples):
        ids = jnp.broadcast_to(token_ref[s : s + 1, :].astype(F32), (8, rows)).T[:, :1]
        one_hot = (ids == iota((rows, vocab), 1, F32)).astype(BF16)
        out_ref[s] = dot(one_hot, table_ref[...]).astype(BF16)


def gate_kernel(
    far_ref, own_ref, rate_ref, base_ref, query_ref, gated_ref, sum_ref, squares
):
    samples, rows, width = query_ref.shape
    height = (base_ref.shape[0] - samples * rows) // 2
    modes = own_ref.shape[0] // samples
    copies = sum_ref.shape[0]
    own = iota((LANES, LANES), 0) // modes == iota((LANES, LANES), 1) // GROUP
    for tile in range(width // LANES):
        lanes = slice(tile * LANES, (tile + 1) * LANES)
        rate = rate_ref[:, lanes]
        head = jnp.exp(-rate * (1.0 + iota((LANES, 1), 0, F32)))
        step = jnp.exp(-rate * float(LANES))
        after = [head]
        for _ in range(rows // LANES - 1):
            after.append(after[-1] * step)
        upper, lower = halves(jnp.concatenate(after, axis=0))
        after = jnp.concatenate([upper, lower, upper], axis=1)
        factors = base_ref[samples * rows :, lanes].astype(F32)
        factors = factors[:height] + factors[height:]
        for s in range(samples):
            carried = own_ref[s * modes : (s + 1) * modes, lanes]
            for first in range(s * modes, far_ref.shape[0], samples * modes):
                carried = carried + far_ref[first : first + modes, lanes].astype(F32)
            early = factors[(s + 2) * modes : (s + 3) * modes]
            state = (factors[:modes] * carried + early) * factors[modes : 2 * modes]
            spread = jnp.concatenate([state] * TILE_GROUPS, axis=0)
            upper, lower = halves(jnp.where(own, spread, 0.0))
            carry = dot(after, jnp.concatenate([upper, upper, lower], axis=0))
            base = base_ref[s * rows : (s + 1) * rows, lanes].astype(F32)
            gated = query_ref[s, :, lanes].astype(F32) * (base + carry)
            gated_ref[s, :, lanes] = gated
            if tile == 0:
                squares[s] = gated * gated
            else:
                squares[s] = squares[s] + gated * gated
    for s in range(samples):
        total = jnp.sum(squares[s].T, axis=0, keepdims=True)
        sum_ref[:, :, s * rows : (s + 1) * rows] = jnp.broadcast_to(
            total.reshape(1, 1, rows), (copies, 1, rows)
        )


def norm_kernel(
    length_ref, index_ref, sum_ref, gated_ref, embed_ref, gain_ref, out_target, out_ref, left, *, full
):
    samples, rows, _ = gated_ref.shape
    here = 128
    total = jnp.sum(sum_ref[...], axis=0)
    scale = jnp.broadcast_to(lax.rsqrt(total / full + 1e-06), (8, samples * rows)).T[:, :1]
    stores = []
    for s in range(samples):
        for part in range(rows // here):
            at = slice(part * here, (part + 1) * here)
            start = index_ref[0] * rows + part * here
            valid = start + iota((here, 1), 0) < length_ref[s]
            first = s * rows + part * here
            value = gated_ref[s, at, :] * scale[first : first + here] * gain_ref[...]
            value = value + embed_ref[s, at, :].astype(F32)
            out_ref[s, at, :] = jnp.where(valid, value, 0.0).astype(BF16)
            store = pltpu.make_async_copy(
                out_ref.at[s, at, :], out_target.at[s, at, :], left.at[s, part]
            )
            store.start()
            stores.append(store)
    for store in stores:
        store.wait()


def params(mebibytes):
    return pltpu.CompilerParams(vmem_limit_bytes=int(mebibytes * (1 << 20)))


def per_device(
    token_ids,
    lengths,
    embedding,
    query_act,
    key_act,
    value_act,
    short_filter,
    decay_rates,
    residues,
    skip_gain,
    norm_gain,
):
    samples, rows, width = query_act.shape
    taps = short_filter.shape[1]
    groups, modes = decay_rates.shape
    vocab = embedding.shape[0]
    chunks = lax.axis_size("ctx")
    columns = lax.axis_size("tp")
    index = lax.axis_index("ctx").reshape(1)
    tiles = width // LANES
    smem = pl.BlockSpec(memory_space=pltpu.SMEM)

    def cube():
        return pl.BlockSpec((samples, rows, LANES), lambda i: (0, 0, i))

    def flat(height):
        return pl.BlockSpec((height, LANES), lambda i: (0, i))

    def grouped(cols):
        return pl.BlockSpec((TILE_GROUPS, cols), lambda i: (i, 0))

    state_rows = samples * modes
    border_rows = samples * taps + 2 * state_rows
    base_rows = samples * rows + 2 * (2 * modes + state_rows)
    shape = jax.ShapeDtypeStruct
    whole = pl.BlockSpec((modes, groups), lambda i: (0, 0))
    rates = decay_rates.T
    near = 8 if chunks % 16 == 0 else 2
    far = chunks // near
    near_groups = [[g * near + i for i in range(near)] for g in range(far)]
    far_groups = [[g * near + i for g in range(far)] for i in range(near)]

    def exchange(blocks, groups):
        return lax.all_to_all(
            blocks, "ctx", split_axis=0, concat_axis=0, axis_index_groups=groups, tiled=True
        )


    vmem = pl.BlockSpec(memory_space=pltpu.VMEM)
    anywhere = pl.BlockSpec(memory_space=pl.ANY)

    def states_step(*refs):
        states_kernel(*refs, taps=taps)

    states, border = pl.pallas_call(
        states_step,
        in_specs=[anywhere, anywhere, anywhere],
        out_specs=[anywhere, anywhere],
        out_shape=[
            shape((near * state_rows, width), BF16),
            shape((border_rows, width), BF16),
        ],
        scratch_shapes=[
            pltpu.VMEM((modes, groups), F32),
            pltpu.VMEM((samples, rows, width), BF16),
            pltpu.VMEM((samples, rows, width), BF16),
            pltpu.VMEM((near * state_rows, width), BF16),
            pltpu.VMEM((border_rows, width), BF16),
            pltpu.SemaphoreType.DMA((1,)),
            pltpu.SemaphoreType.DMA((2, tiles)),
            pltpu.SemaphoreType.DMA((2, tiles)),
        ],
        compiler_params=params(60),
        name="states",
    )(rates, key_act, value_act)
    before = lax.ppermute(border, "ctx", [(i, i + 1) for i in range(chunks - 1)])
    gathered = exchange(states, near_groups)

    embedded = pl.pallas_call(
        embed_kernel,
        out_shape=shape((samples, rows, width), BF16),
        cost_estimate=pl.CostEstimate(
            flops=2 * samples * rows * width * vocab, bytes_accessed=4 << 20, transcendentals=0
        ),
        compiler_params=params(16),
        name="embed",
    )(token_ids, embedding)

    base = pl.pallas_call(
        local_kernel,
        grid=(tiles,),
        in_specs=[flat(border_rows), cube(), cube(), grouped(taps), whole, whole, flat(1)],
        out_specs=flat(base_rows),
        out_shape=shape((base_rows, width), BF16),
        scratch_shapes=[
            pltpu.VMEM((samples, LANES, rows + 2 * taps), BF16),
            pltpu.VMEM((samples, LANES, 2 * rows), BF16),
            pltpu.VMEM((samples, LANES, rows), F32),
        ],
        cost_estimate=pl.CostEstimate(
            flops=12_000_000_000, bytes_accessed=8 << 20, transcendentals=1 << 20
        ),
        compiler_params=params(48),
        name="local",
    )(
        before,
        key_act,
        value_act,
        short_filter,
        rates,
        residues.T,
        skip_gain.reshape(1, width),
    )

    def group_step(*refs):
        group_kernel(*refs, near=near, rows=rows)

    sent, own = pl.pallas_call(
        group_step,
        in_specs=[smem, vmem, vmem],
        out_shape=[shape((far * state_rows, width), BF16), shape((state_rows, width), F32)],
        compiler_params=params(8),
        name="group",
    )(index, jnp.repeat(rates, GROUP, axis=1), gathered)
    carried = exchange(sent, far_groups)

    gated, sums = pl.pallas_call(
        gate_kernel,
        out_shape=[
            shape((samples, rows, width), F32),
            shape((columns, 1, samples * rows), F32),
        ],
        scratch_shapes=[
            pltpu.VMEM((samples, rows, LANES), F32),
        ],
        compiler_params=params(16),
        name="gate",
    )(carried, own, decay_rates.reshape(1, groups * modes), base, query_act)
    shares = lax.all_to_all(sums, "tp", split_axis=0, concat_axis=0, tiled=True)

    def norm(*refs):
        norm_kernel(*refs, full=float(columns * width))

    return pl.pallas_call(
        norm,
        in_specs=[smem, smem, vmem, vmem, vmem, vmem],
        out_specs=anywhere,
        out_shape=shape((samples, rows, width), BF16),
        scratch_shapes=[
            pltpu.VMEM((samples, rows, width), BF16),
            pltpu.SemaphoreType.DMA((samples, rows // 128)),
        ],
        compiler_params=params(16),
        name="norm",
    )(lengths, index, shares, gated, embedded, norm_gain.reshape(1, width))


def solution(mesh):
    placed = (
        P(None, "ctx"),
        P(),
        P(None, "tp"),
        P(None, "ctx", "tp"),
        P(None, "ctx", "tp"),
        P(None, "ctx", "tp"),
        P("tp", None),
        P("tp", None),
        P("tp", None),
        P("tp"),
        P("tp"),
    )
    return jax.shard_map(
        per_device, mesh=mesh, in_specs=placed, out_specs=P(None, "ctx", "tp"), check_vma=False
    )
```

```python
import jax
import jax.numpy as jnp
from jax import lax
from jax.experimental import pallas as pl
from jax.experimental.pallas import tpu as pltpu
from jax.sharding import PartitionSpec as P

GROUP = 16
LANES = 128
TILE_GROUPS = LANES // GROUP
F32 = jnp.float32
BF16 = jnp.bfloat16


def iota(shape, dim, dtype=jnp.int32):
    return lax.broadcasted_iota(jnp.int32, shape, dim).astype(dtype)


def own_group(stacked, rows):
    lane_group = iota((rows, LANES), 1) // GROUP
    picked = stacked[:rows]
    for g in range(1, TILE_GROUPS):
        picked = jnp.where(lane_group == g, stacked[g * rows : (g + 1) * rows], picked)
    return picked


def halves(values):
    upper = values.astype(BF16)
    return upper, (values - upper.astype(F32)).astype(BF16)


def dot(a, b):
    return jnp.dot(a, b, preferred_element_type=F32)


def tile_column(table, tile):
    modes, groups = table.shape
    parts = []
    for g in range(TILE_GROUPS):
        here = iota((modes, groups), 1) == tile * TILE_GROUPS + g
        parts.append(jnp.sum(jnp.where(here, table, 0.0), axis=1, keepdims=True))
    return jnp.concatenate(parts, axis=0)


def product_of(key, value):
    return (key.astype(F32) * value.astype(F32)).astype(BF16)


def states_kernel(
    rate_source,
    key_source,
    value_source,
    state_target,
    border_target,
    rate_ref,
    key_ref,
    value_ref,
    state_ref,
    border_ref,
    ready,
    arrived,
    left,
    *,
    taps,
):
    samples, rows, width = key_ref.shape
    modes = rate_ref.shape[0]
    tiles = [slice(first, first + LANES) for first in range(0, width, LANES)]
    rate_load = pltpu.make_async_copy(rate_source, rate_ref, ready.at[0])
    rate_load.start()
    loads, stores = [], []
    for tile, lanes in enumerate(tiles):
        pair = (
            pltpu.make_async_copy(
                key_source.at[:, :, lanes], key_ref.at[:, :, lanes], arrived.at[0, tile]
            ),
            pltpu.make_async_copy(
                value_source.at[:, :, lanes], value_ref.at[:, :, lanes], arrived.at[1, tile]
            ),
        )
        for load in pair:
            load.start()
        loads.append(pair)
    rate_load.wait()
    tables = []
    for tile in range(len(tiles)):
        groups = range(tile * TILE_GROUPS, (tile + 1) * TILE_GROUPS)
        rate = jnp.concatenate([rate_ref[:, g : g + 1] for g in groups], axis=0)
        weights = [jnp.exp(-rate * (taps - 1.0 - iota((1, taps), 1, F32)))]
        step = jnp.exp(-rate * float(taps))
        for _ in range(rows // taps - 1):
            weights.insert(0, weights[0] * step)
        tables.append(jnp.concatenate(halves(jnp.concatenate(weights, axis=1)), axis=0))
    for tile, lanes in enumerate(tiles):
        weights = tables[tile]
        half = weights.shape[0] // 2
        for load in loads[tile]:
            load.wait()
        for s in range(samples):
            product = product_of(key_ref[s, :, lanes], value_ref[s, :, lanes])
            full = dot(weights, product)
            state = own_group(full[:half] + full[half:], modes)
            state = state.astype(BF16)
            for copy in range(state_ref.shape[0] // (samples * modes)):
                at = (copy * samples + s) * modes
                state_ref[at : at + modes, lanes] = state
            border_ref[s * taps : (s + 1) * taps, lanes] = product[rows - taps :]
            early = dot(weights[:, taps:], product[: rows - taps])
            upper, lower = halves(own_group(early[:half] + early[half:], modes))
            first = samples * taps + s * modes
            border_ref[first : first + modes, lanes] = upper
            border_ref[first + samples * modes : first + (samples + 1) * modes, lanes] = lower
        pair = (
            pltpu.make_async_copy(
                state_ref.at[:, lanes], state_target.at[:, lanes], left.at[0, tile]
            ),
            pltpu.make_async_copy(
                border_ref.at[:, lanes], border_target.at[:, lanes], left.at[1, tile]
            ),
        )
        for store in pair:
            store.start()
            stores.append(store)
    for store in stores:
        store.wait()


def group_kernel(index_ref, rate_ref, state_ref, far_ref, own_ref, *, near, rows):
    height = own_ref.shape[0]
    far = far_ref.shape[0] // height
    modes = rate_ref.shape[0]
    group, place = index_ref[0] // near, lax.rem(index_ref[0], near)
    rate = jnp.concatenate([rate_ref[...]] * (height // modes), axis=0) * float(rows)
    decay = jnp.exp(-rate)
    held = jnp.zeros(own_ref.shape, F32)
    own, short = held, held
    for p in range(near):
        own = jnp.where(place == p + 1, held, own)
        short = held
        held = decay * held + state_ref[p * height : (p + 1) * height, :].astype(F32)
    own_ref[...] = own
    for other in range(far):
        ahead = (other - group) * near + place - near - 1
        weight = jnp.exp(-rate * jnp.maximum(ahead, 0).astype(F32))
        value = jnp.where(ahead < 0, short, weight * held)
        value = jnp.where(other > group, value, 0.0)
        far_ref[other * height : (other + 1) * height, :] = value.astype(BF16)


def dot_rows(a, b):
    return lax.dot_general(a, b, (((1,), (1,)), ((), ())), preferred_element_type=F32)


def local_kernel(
    border_ref,
    key_ref,
    value_ref,
    filter_ref,
    rate_ref,
    residue_ref,
    skip_ref,
    base_ref,
    product_window,
    mixed_window,
    turned,
):
    samples, rows, _ = key_ref.shape
    modes = rate_ref.shape[0]
    taps = filter_ref.shape[1]
    span = rows + taps
    blocks = rows // taps
    before = span - 2 * taps
    tile = pl.program_id(0)
    rate = tile_column(rate_ref[...], tile)
    residue = tile_column(residue_ref[...], tile)
    filters = filter_ref[...]

    reverse = (iota((taps, 2 * taps), 0) + iota((taps, 2 * taps), 1) == taps).astype(BF16)
    short_base = dot(filters, reverse)
    wide = span + taps
    place = iota((1, wide), 1)
    lag = jnp.where(place <= rows, rows - place, rows + wide - place)
    zero = jnp.logical_and(place > rows, place <= span)
    modal = residue * jnp.exp(-rate * lag.astype(F32))
    modal = jnp.where(zero, 0.0, modal)
    long_base = jnp.sum(modal.reshape(TILE_GROUPS, modes, wide), axis=1)

    for s in range(samples):
        product_window[s, :, :taps] = jnp.zeros((LANES, taps), BF16)
        mixed_window[s, :, :before] = jnp.zeros((LANES, before), BF16)
        border = border_ref[s * taps : (s + 1) * taps, :].astype(F32)
        product_window[s, :, taps : 2 * taps] = border.T.astype(BF16)
        product = product_of(key_ref[s], value_ref[s]).astype(F32)
        product_window[s, :, 2 * taps :] = product.T.astype(BF16)

    skip = jnp.broadcast_to(skip_ref[...], (8, LANES)).T[:, :1]
    for g in range(TILE_GROUPS):
        channels = slice(g * GROUP, (g + 1) * GROUP)
        spread = jnp.broadcast_to(short_base[g : g + 1], (taps, 2 * taps))
        short_table = pltpu.roll(spread, 0, 1, stride=1, stride_axis=0).astype(BF16)
        pieces = [
            product_window[s, channels, b * taps : (b + 2) * taps]
            for s in range(samples)
            for b in range(blocks + 1)
        ]
        mixed = dot_rows(jnp.concatenate(pieces, axis=0), short_table).astype(BF16)
        for s in range(samples):
            for b in range(blocks + 1):
                first = (s * (blocks + 1) + b) * GROUP
                mixed_window[s, channels, before + b * taps : before + (b + 1) * taps] = mixed[
                    first : first + GROUP
                ]
        spread = jnp.broadcast_to(long_base[g : g + 1], (taps, wide))
        long_table = pltpu.roll(spread, 0, 1, stride=1, stride_axis=0)[:, :span].astype(BF16)
        pieces = [
            mixed_window[s, channels, b * taps : b * taps + span]
            for s in range(samples)
            for b in range(blocks)
        ]
        filtered = dot_rows(jnp.concatenate(pieces, axis=0), long_table)
        for s in range(samples):
            for b in range(blocks):
                first = (s * blocks + b) * GROUP
                at = (s * (blocks + 1) + b + 1) * GROUP
                turned[s, channels, b * taps : (b + 1) * taps] = filtered[
                    first : first + GROUP
                ] + skip[channels] * mixed[at : at + GROUP].astype(F32)
    for s in range(samples):
        base_ref[s * rows : (s + 1) * rows, :] = turned[s].T.astype(BF16)

    tap_weights = jnp.exp(-rate * (taps - iota((1, taps), 1, F32)))
    spread = jnp.broadcast_to(
        filters.astype(F32)[:, None, :], (TILE_GROUPS, modes, taps)
    ).reshape(TILE_GROUPS * modes, taps)
    gain = residue * jnp.sum(spread * tap_weights, axis=1, keepdims=True)
    square = (TILE_GROUPS * modes, LANES)
    decay = own_group(jnp.broadcast_to(jnp.exp(-rate * float(rows - taps)), square), modes)
    gain = own_group(jnp.broadcast_to(gain, square), modes)
    first, state_rows = samples * taps, samples * modes
    early = border_ref[first : first + state_rows, :].astype(F32)
    early = early + border_ref[first + state_rows :, :].astype(F32)
    factors = jnp.concatenate([decay, gain, early], axis=0)
    base_ref[samples * rows :, :] = jnp.concatenate(halves(factors), axis=0)


def embed_kernel(token_ref, table_ref, out_ref):
    samples, rows = token_ref.shape
    vocab = table_ref.shape[0]
    for s in range(samples):
        ids = jnp.broadcast_to(token_ref[s : s + 1, :].astype(F32), (8, rows)).T[:, :1]
        one_hot = (ids == iota((rows, vocab), 1, F32)).astype(BF16)
        out_ref[s] = dot(one_hot, table_ref[...]).astype(BF16)


def gate_kernel(
    far_ref, own_ref, rate_ref, base_ref, query_ref, gated_ref, sum_ref, squares
):
    samples, rows, width = query_ref.shape
    height = (base_ref.shape[0] - samples * rows) // 2
    modes = own_ref.shape[0] // samples
    copies = sum_ref.shape[0]
    own = iota((LANES, LANES), 0) // modes == iota((LANES, LANES), 1) // GROUP
    for tile in range(width // LANES):
        lanes = slice(tile * LANES, (tile + 1) * LANES)
        rate = rate_ref[:, lanes]
        head = jnp.exp(-rate * (1.0 + iota((LANES, 1), 0, F32)))
        step = jnp.exp(-rate * float(LANES))
        after = [head]
        for _ in range(rows // LANES - 1):
            after.append(after[-1] * step)
        upper, lower = halves(jnp.concatenate(after, axis=0))
        after = jnp.concatenate([upper, lower, upper], axis=1)
        factors = base_ref[samples * rows :, lanes].astype(F32)
        factors = factors[:height] + factors[height:]
        for s in range(samples):
            carried = own_ref[s * modes : (s + 1) * modes, lanes]
            for first in range(s * modes, far_ref.shape[0], samples * modes):
                carried = carried + far_ref[first : first + modes, lanes].astype(F32)
            early = factors[(s + 2) * modes : (s + 3) * modes]
            state = (factors[:modes] * carried + early) * factors[modes : 2 * modes]
            spread = jnp.concatenate([state] * TILE_GROUPS, axis=0)
            upper, lower = halves(jnp.where(own, spread, 0.0))
            carry = dot(after, jnp.concatenate([upper, upper, lower], axis=0))
            base = base_ref[s * rows : (s + 1) * rows, lanes].astype(F32)
            gated = query_ref[s, :, lanes].astype(F32) * (base + carry)
            gated_ref[s, :, lanes] = gated.astype(BF16)
            if tile == 0:
                squares[s] = gated * gated
            else:
                squares[s] = squares[s] + gated * gated
    for s in range(samples):
        total = jnp.sum(squares[s].T, axis=0, keepdims=True)
        sum_ref[:, :, s * rows : (s + 1) * rows] = jnp.broadcast_to(
            total.reshape(1, 1, rows), (copies, 1, rows)
        )


def norm_kernel(
    length_ref, index_ref, sum_ref, gated_ref, embed_ref, gain_ref, out_target, out_ref, left, *, full
):
    samples, rows, _ = gated_ref.shape
    here = 128
    total = jnp.sum(sum_ref[...], axis=0)
    scale = jnp.broadcast_to(lax.rsqrt(total / full + 1e-06), (8, samples * rows)).T[:, :1]
    stores = []
    for s in range(samples):
        for part in range(rows // here):
            at = slice(part * here, (part + 1) * here)
            start = index_ref[0] * rows + part * here
            valid = start + iota((here, 1), 0) < length_ref[s]
            first = s * rows + part * here
            value = gated_ref[s, at, :].astype(F32) * scale[first : first + here] * gain_ref[...]
            value = value + embed_ref[s, at, :].astype(F32)
            out_ref[s, at, :] = jnp.where(valid, value, 0.0).astype(BF16)
            store = pltpu.make_async_copy(
                out_ref.at[s, at, :], out_target.at[s, at, :], left.at[s, part]
            )
            store.start()
            stores.append(store)
    for store in stores:
        store.wait()


def params(mebibytes):
    return pltpu.CompilerParams(vmem_limit_bytes=int(mebibytes * (1 << 20)))


def per_device(
    token_ids,
    lengths,
    embedding,
    query_act,
    key_act,
    value_act,
    short_filter,
    decay_rates,
    residues,
    skip_gain,
    norm_gain,
):
    samples, rows, width = query_act.shape
    taps = short_filter.shape[1]
    groups, modes = decay_rates.shape
    vocab = embedding.shape[0]
    chunks = lax.axis_size("ctx")
    columns = lax.axis_size("tp")
    index = lax.axis_index("ctx").reshape(1)
    tiles = width // LANES
    smem = pl.BlockSpec(memory_space=pltpu.SMEM)

    def cube():
        return pl.BlockSpec((samples, rows, LANES), lambda i: (0, 0, i))

    def flat(height):
        return pl.BlockSpec((height, LANES), lambda i: (0, i))

    def grouped(cols):
        return pl.BlockSpec((TILE_GROUPS, cols), lambda i: (i, 0))

    state_rows = samples * modes
    border_rows = samples * taps + 2 * state_rows
    base_rows = samples * rows + 2 * (2 * modes + state_rows)
    shape = jax.ShapeDtypeStruct
    whole = pl.BlockSpec((modes, groups), lambda i: (0, 0))
    rates = decay_rates.T
    near = 8 if chunks % 16 == 0 else 2
    far = chunks // near
    near_groups = [[g * near + i for i in range(near)] for g in range(far)]
    far_groups = [[g * near + i for g in range(far)] for i in range(near)]

    def exchange(blocks, groups):
        return lax.all_to_all(
            blocks, "ctx", split_axis=0, concat_axis=0, axis_index_groups=groups, tiled=True
        )


    vmem = pl.BlockSpec(memory_space=pltpu.VMEM)
    anywhere = pl.BlockSpec(memory_space=pl.ANY)

    def states_step(*refs):
        states_kernel(*refs, taps=taps)

    states, border = pl.pallas_call(
        states_step,
        in_specs=[anywhere, anywhere, anywhere],
        out_specs=[anywhere, anywhere],
        out_shape=[
            shape((near * state_rows, width), BF16),
            shape((border_rows, width), BF16),
        ],
        scratch_shapes=[
            pltpu.VMEM((modes, groups), F32),
            pltpu.VMEM((samples, rows, width), BF16),
            pltpu.VMEM((samples, rows, width), BF16),
            pltpu.VMEM((near * state_rows, width), BF16),
            pltpu.VMEM((border_rows, width), BF16),
            pltpu.SemaphoreType.DMA((1,)),
            pltpu.SemaphoreType.DMA((2, tiles)),
            pltpu.SemaphoreType.DMA((2, tiles)),
        ],
        compiler_params=params(60),
        name="states",
    )(rates, key_act, value_act)
    before = lax.ppermute(border, "ctx", [(i, i + 1) for i in range(chunks - 1)])
    gathered = exchange(states, near_groups)

    embedded = pl.pallas_call(
        embed_kernel,
        out_shape=shape((samples, rows, width), BF16),
        cost_estimate=pl.CostEstimate(
            flops=2 * samples * rows * width * vocab, bytes_accessed=4 << 20, transcendentals=0
        ),
        compiler_params=params(16),
        name="embed",
    )(token_ids, embedding)

    base = pl.pallas_call(
        local_kernel,
        grid=(tiles,),
        in_specs=[flat(border_rows), cube(), cube(), grouped(taps), whole, whole, flat(1)],
        out_specs=flat(base_rows),
        out_shape=shape((base_rows, width), BF16),
        scratch_shapes=[
            pltpu.VMEM((samples, LANES, rows + 2 * taps), BF16),
            pltpu.VMEM((samples, LANES, 2 * rows), BF16),
            pltpu.VMEM((samples, LANES, rows), F32),
        ],
        cost_estimate=pl.CostEstimate(
            flops=12_000_000_000, bytes_accessed=8 << 20, transcendentals=1 << 20
        ),
        compiler_params=params(60),
        name="local",
    )(
        before,
        key_act,
        value_act,
        short_filter,
        rates,
        residues.T,
        skip_gain.reshape(1, width),
    )

    def group_step(*refs):
        group_kernel(*refs, near=near, rows=rows)

    sent, own = pl.pallas_call(
        group_step,
        in_specs=[smem, vmem, vmem],
        out_shape=[shape((far * state_rows, width), BF16), shape((state_rows, width), F32)],
        compiler_params=params(8),
        name="group",
    )(index, jnp.repeat(rates, GROUP, axis=1), gathered)
    carried = exchange(sent, far_groups)

    gated, sums = pl.pallas_call(
        gate_kernel,
        out_shape=[
            shape((samples, rows, width), BF16),
            shape((columns, 1, samples * rows), F32),
        ],
        scratch_shapes=[
            pltpu.VMEM((samples, rows, LANES), F32),
        ],
        compiler_params=params(16),
        name="gate",
    )(carried, own, decay_rates.reshape(1, groups * modes), base, query_act)
    shares = lax.all_to_all(sums, "tp", split_axis=0, concat_axis=0, tiled=True)

    def norm(*refs):
        norm_kernel(*refs, full=float(columns * width))

    return pl.pallas_call(
        norm,
        in_specs=[smem, smem, vmem, vmem, vmem, vmem],
        out_specs=anywhere,
        out_shape=shape((samples, rows, width), BF16),
        scratch_shapes=[
            pltpu.VMEM((samples, rows, width), BF16),
            pltpu.SemaphoreType.DMA((samples, rows // 128)),
        ],
        compiler_params=params(16),
        name="norm",
    )(lengths, index, shares, gated, embedded, norm_gain.reshape(1, width))


def solution(mesh):
    placed = (
        P(None, "ctx"),
        P(),
        P(None, "tp"),
        P(None, "ctx", "tp"),
        P(None, "ctx", "tp"),
        P(None, "ctx", "tp"),
        P("tp", None),
        P("tp", None),
        P("tp", None),
        P("tp"),
        P("tp"),
    )
    return jax.shard_map(
        per_device, mesh=mesh, in_specs=placed, out_specs=P(None, "ctx", "tp"), check_vma=False
    )
```
